256 devices in a mesh: seg: 32 (over x, z), term: 8 (over y, core).
Axes of the slice: x: 4, y: 4, z: 8, core: 2. Of those that a mesh axis runs over, the one named last changes fastest.
Arguments:
- left_blocks: bfloat16 [32, 32, 512, 512], P('seg', 'term'), may hold values from -0.25 to 0.25
- right_blocks: bfloat16 [32, 32, 512, 512], P('seg', 'term'), may hold values from -0.046875 to 0.046875
- start_state: float32 [32, 512, 512], P('seg'), may hold values from -6 to 6
- left_transfer: float32 [32, 512, 512], P('seg'), as said below
- right_transfer: float32 [32, 512, 512], P('seg'), as said below
- ranks: int32 [32, 2], P('seg'), may hold values from 128 to 512
Outputs:
- final_state: float32 [32, 512, 512], P('seg')
The draws below stay inside these ranges and needn't reach their ends.
Inputs may be any that keep to these rules, and one draw needn't show every extreme that they name: `left_transfer`: entries of size about 0.3 / sqrt(512). `right_transfer`: entries of size about 0.3 / sqrt(512).
All inputs are finite; a program needn't handle non-finite values.
Results may differ from the reference program's by a relative error of at most 0.008.
Values may be sent and summed in bfloat16 or wider, within the bound.
A program may use at most 128 MiB of HBM per device.

```python
import jax
import jax.numpy as jnp
from jax import lax

BLK = 512
ITERS = 2
TERMS = 32
NSEGS = 32


def scaled_part(raw):
    return 0.3 * raw / jnp.sqrt(1.0 * BLK)


def draw_left_transfer(key, part):
    key = jax.random.fold_in(key, 1)
    raw = jnp.clip(jax.random.normal(key, (NSEGS, BLK, BLK), jnp.float32), -6.0, 6.0)
    return scaled_part(raw)


def draw_right_transfer(key, part):
    key = jax.random.fold_in(key, 2)
    raw = jnp.clip(jax.random.normal(key, (NSEGS, BLK, BLK), jnp.float32), -6.0, 6.0)
    return scaled_part(raw)


def draw_ranks(key, part):
    key = jax.random.fold_in(key, 3)
    values = jax.random.randint(key, (NSEGS, 2), BLK // 4, BLK + 1, dtype=jnp.int32)
    chosen = jax.random.randint(jax.random.fold_in(key, 7), (), 0, NSEGS, dtype=jnp.int32)
    values = values.at[chosen, 0].set(BLK)
    values = values.at[(chosen + 1) % NSEGS, 1].set(BLK // 4)
    return values


def block_scale(rng, shape, shards, least, top_value):
    gain = 1.0
    for axis_at, shards_of in shards:
        draws = jax.random.uniform(jax.random.fold_in(jax.random.fold_in(rng, 6), axis_at), (shards_of,), jnp.float32, least / len(shards), top_value / len(shards))
        gain = gain * jnp.repeat(jnp.exp(draws), shape[axis_at] // shards_of).reshape((-1,) + (1,) * (len(shape) - 1 - axis_at))
    return gain


def scatter_about(own_key, dims, deviation, bound, pieces=(), held_as=jnp.bfloat16):
    gain = block_scale(own_key, dims, pieces, -0.22, 0.18) if pieces else 1.0
    entries = jax.random.normal(own_key, dims, jnp.float32) * deviation * gain
    return jnp.minimum(jnp.maximum(entries, -bound), bound).astype(held_as)


def setup_inputs(seed: int = 0) -> dict:
    key_list = jax.random.split(jax.random.key(seed), 7)
    return {
        "left_blocks": scatter_about(key_list[0], (NSEGS, TERMS, BLK, BLK), BLK ** -0.5, 0.25, ((0, 32), (1, 8))),
        "right_blocks": scatter_about(key_list[1], (NSEGS, TERMS, BLK, BLK), (BLK * TERMS) ** -0.5, 0.046875, ((0, 32), (1, 8))),
        "start_state": scatter_about(key_list[2], (NSEGS, BLK, BLK), 1.0, 6.0, ((0, 32),), jnp.float32),
        "left_transfer": draw_left_transfer(jax.random.fold_in(key_list[6], 71), 0),
        "right_transfer": draw_right_transfer(jax.random.fold_in(key_list[6], 71), 0),
        "ranks": draw_ranks(jax.random.fold_in(key_list[6], 71), 0),
    }


def normed(block, target):
    return block * (target / jnp.sqrt(jnp.sum(block * block) + 1e-06))

def env_table(transfer, backward):
    unit_matrix = jnp.eye(BLK, dtype=jnp.float32)
    root = float(BLK) ** 0.5
    units = jax.vmap(lambda gen: normed(unit_matrix + gen, root))(transfer)

    def advance(carry, member):
        nxt = normed(jnp.dot(carry, member, precision=lax.Precision.HIGHEST), root)
        return (nxt, carry)
    final_carry, table = lax.scan(advance, unit_matrix, units, reverse=backward)
    return table

def make_mask(rank_pair):
    rows_live = (jnp.arange(BLK) < rank_pair[0]).astype(jnp.float32)
    cols_live = (jnp.arange(BLK) < rank_pair[1]).astype(jnp.float32)
    return rows_live[:, None] * cols_live[None, :]

def first_half(inputs):
    left_ops, right_ops, basis, start, rank_pair = inputs
    live_mask = make_mask(rank_pair)
    basis_b = basis.astype(jnp.bfloat16)
    basis_wide = basis_b.astype(jnp.float32)
    state = normed(start * live_mask, float(BLK))
    for step_index in range(ITERS):
        state_b = state.astype(jnp.bfloat16)
        moved = jnp.dot(basis_b, state_b, preferred_element_type=jnp.float32).astype(jnp.bfloat16)
        inner = jnp.einsum('tij,jk->tik', left_ops.astype(jnp.float32), moved.astype(jnp.float32)).astype(jnp.bfloat16)
        summed = jnp.einsum('tik,tlk->il', inner.astype(jnp.float32), right_ops.astype(jnp.float32))
        applied = jnp.dot(basis_wide.T, summed, precision=lax.Precision.HIGHEST)
        state = normed((2.0 * state - applied) * live_mask, float(BLK))
    return state

def second_half(inputs):
    left_ops, right_ops, basis, start, rank_pair = inputs
    live_mask = make_mask(rank_pair)
    basis_b = basis.astype(jnp.bfloat16)
    basis_wide = basis_b.astype(jnp.float32)
    state = normed(start * live_mask, float(BLK))
    for step_index in range(ITERS):
        state_b = state.astype(jnp.bfloat16)
        moved = jnp.dot(state_b, basis_b, preferred_element_type=jnp.float32).astype(jnp.bfloat16)
        outer = jnp.einsum('ik,tlk->til', moved.astype(jnp.float32), right_ops.astype(jnp.float32)).astype(jnp.bfloat16)
        summed = jnp.einsum('tji,til->jl', left_ops.astype(jnp.float32), outer.astype(jnp.float32))
        applied = jnp.dot(summed, basis_wide.T, precision=lax.Precision.HIGHEST)
        state = normed((2.0 * state - applied) * live_mask, float(BLK))
    return state

def reference(left_blocks, right_blocks, start_state, left_transfer, right_transfer, ranks):
    left_env = env_table(left_transfer, False)
    right_env = env_table(right_transfer, True)
    first_state = lax.map(first_half, (left_blocks, right_blocks, left_env, start_state, ranks))
    neighbour = jnp.concatenate([jnp.zeros((1, BLK, BLK), jnp.bfloat16), first_state[:-1].astype(jnp.bfloat16)], axis=0)
    seeded = first_state + 0.5 * neighbour.astype(jnp.float32)
    return lax.map(second_half, (left_blocks, right_blocks, right_env, seeded, ranks))
```

```python
import functools

import jax
import jax.numpy as jnp
from jax import lax
from jax.experimental import pallas as pl
from jax.experimental.pallas import tpu as pltpu
from jax.sharding import PartitionSpec as P

MESH = pl.DeviceIdType.MESH
BF = jnp.bfloat16
F32 = jnp.float32
EPS = 1e-06
ITERS = 2
NY = 4


def dot_ab(a, b):
    return jnp.dot(a, b, preferred_element_type=F32)


def dot_abt(a, b):
    return lax.dot_general(a, b, (((1,), (1,)), ((), ())), preferred_element_type=F32)


def kernel(
    nseg, blk, terms,
    left_hbm, right_hbm, start_hbm, lt_hbm, rt_hbm, ranks, out_ref,
    ops, tr, st, unit, hop, win, env, env_scale, gath, inner, own, s1_out, s1_in, s2_out, s2_in,
    state, part, state_all, part_all, near_out, near_in,
    in_sem, hop_ss, hop_rs, win_ss, win_rs, env_ss, env_rs, gath_ss, gath_rs, all_ss, all_rs, sum_ss, sum_rs,
    s1_sem, s2_ss, s2_rs, near_sem,
):
    levels = nseg.bit_length() - 1
    seg, term = lax.axis_index("seg"), lax.axis_index("term")
    y, core = lax.div(term, 2), lax.rem(term, 2)
    sign = 1 - 2 * core
    place = jnp.where(core == 0, seg, nseg - 1 - seg)
    half, wide, slim = blk // 2, blk // NY, blk // (2 * NY)
    buddy = (seg, term + sign)

    def along(by):
        return (lax.rem(seg + sign * by + 2 * nseg, nseg), term)

    def chip(by):
        return (seg, lax.rem(y + by, NY) * 2 + core)

    def rows(index, size):
        return pl.ds(pl.multiple_of(index * size, size), size)

    def remote(src, dst, ss, rs, to):
        return pltpu.make_async_remote_copy(
            src_ref=src, dst_ref=dst, send_sem=ss, recv_sem=rs, device_id=to, device_id_type=MESH
        )

    load_l = pltpu.make_async_copy(left_hbm.at[0], ops.at[0], in_sem.at[0])
    load_r = pltpu.make_async_copy(right_hbm.at[0], ops.at[1], in_sem.at[1])
    load_s = pltpu.make_async_copy(start_hbm.at[0], st, in_sem.at[2])
    load_lt = pltpu.make_async_copy(lt_hbm.at[0], tr, in_sem.at[3])
    load_rt = pltpu.make_async_copy(rt_hbm.at[0], tr, in_sem.at[3])

    @pl.when(core == 0)
    def _():
        load_lt.start()

    @pl.when(core == 1)
    def _():
        load_rt.start()

    load_s.start()
    load_l.start()
    load_r.start()

    barrier = pltpu.get_barrier_semaphore()
    partners = [chip(1), chip(2), chip(3), buddy]
    for k in range(levels):
        partners.append(along(1 << k))
        if (1 << k) * 2 != nseg:
            partners.append(along(-(1 << k)))
    for to in partners:
        pl.semaphore_signal(barrier, inc=1, device_id=to, device_id_type=MESH)
    load_lt.wait()

    root = float(blk) ** 0.5
    at_row = lax.broadcasted_iota(jnp.int32, (slim, blk), 0)
    at_col = lax.broadcasted_iota(jnp.int32, (slim, blk), 1)

    def set_unit(i, _):
        unit[rows(i, slim), :] = tr[rows(i, slim), :].astype(BF)
        return 0

    lax.fori_loop(0, 2 * NY, set_unit, 0)
    pl.semaphore_wait(barrier, len(partners))

    mine = rows(y, wide)

    def came(slot, distance):
        got = hop[slot]
        return jnp.where(place < distance, jnp.zeros_like(got), got)

    step = remote(unit.at[mine], hop.at[0], hop_ss.at[0], hop_rs.at[0], along(1))
    step.start()
    step.wait_recv()
    a = came(0, 1)
    rest_rows = tr[mine, :] + a.astype(F32) + dot_ab(a, unit[...])
    win[0, mine, :] = rest_rows.astype(BF)
    step.wait_send()

    for k in range(1, levels):
        w = win.at[k - 1]
        step = remote(w.at[mine], hop.at[k], hop_ss.at[k], hop_rs.at[k], along(1 << k))
        spread = [
            remote(w.at[mine], w.at[mine], win_ss.at[k - 1, i], win_rs.at[k - 1, i], chip(i + 1))
            for i in range(3)
        ]
        step.start()
        for s in spread:
            s.start()
        step.wait_recv()
        for s in spread:
            s.wait_recv()
        a = came(k, 1 << k)
        rest_rows = rest_rows + a.astype(F32) + dot_ab(a, win[k - 1])
        win[k, mine, :] = rest_rows.astype(BF)
        step.wait_send()
        for s in spread:
            s.wait_send()

    last = levels - 1
    step = remote(win.at[last, mine], hop.at[levels], hop_ss.at[levels], hop_rs.at[levels], along(1))
    step.start()
    step.wait_recv()
    eye_rows = jnp.where(
        lax.broadcasted_iota(jnp.int32, (wide, blk), 0) + y * wide
        == lax.broadcasted_iota(jnp.int32, (wide, blk), 1),
        1.0, 0.0,
    )
    env[core, mine, :] = (eye_rows + came(levels, 1).astype(F32)).astype(BF)
    step.wait_send()

    def fold(load, combine, start):
        def one(i, acc):
            return combine(acc, load(i).reshape(slim // 8, 8, blk))

        return lax.fori_loop(0, 2 * NY, one, jnp.full((8, blk), start, F32))

    def square_sum(load):
        acc = fold(load, lambda acc, v: acc + jnp.sum(v * v, axis=0), 0.0)
        return jnp.sum(acc, axis=(0, 1), keepdims=True)

    def largest(load):
        acc = fold(load, lambda acc, v: jnp.maximum(acc, jnp.max(jnp.abs(v), axis=0)), 0.0)
        return jnp.max(acc, axis=(0, 1), keepdims=True)

    def spread_out(view, ss, rs):
        own_view = view(core, y)
        out = [remote(own_view, own_view, ss.at[i], rs.at[i], chip(i + 1)) for i in range(3)]
        out.append(remote(own_view, own_view, ss.at[3], rs.at[3], buddy))
        for o in out:
            o.start()
        return out

    def pass_on(view, out, ss, rs):
        for i in range(3):
            got = view(core, lax.rem(y + NY - 1 - i, NY))
            out[i].wait_recv()
            fwd = remote(got, got, ss.at[4 + i], rs.at[4 + i], buddy)
            fwd.start()
            out.append(fwd)

    def rest(out):
        for o in out[3:]:
            o.wait_recv()

    def sent(out):
        for o in out:
            o.wait_send()

    env_view = lambda c, yy: env.at[c, rows(yy, wide)]
    out = spread_out(env_view, env_ss, env_rs)
    pass_on(env_view, out, env_ss, env_rs)
    rest(out)
    for h in range(2):
        env_rows = lambda i: env[h, rows(i, slim), :].astype(F32)
        down = 1.0 / jnp.maximum(largest(env_rows), 1e-30)
        norm = down * (root / jnp.sqrt(square_sum(lambda i: env_rows(i) * down) + EPS))
        env_scale[h] = jnp.broadcast_to(norm, (8, 128))
    sent(out)

    slot = core * NY + y
    my_rows = rows(slot, slim)
    other = rows(1 - core, half)
    ours = rows(core, half)

    def masked(x, low, high):
        live = (at_row + slot * slim < low) & (at_col < high)
        return jnp.where(live, x, 0.0)

    def note(line, x):
        part[pl.ds(line, 1), :] = jnp.broadcast_to(jnp.sum(x * x, axis=(0, 1), keepdims=True), (1, 128))

    load_s.wait()
    rank0, rank1 = ranks[0, 0], ranks[0, 1]

    def live_start(i):
        v = st[rows(i, slim), :]
        return jnp.where((at_row + i * slim < rank0) & (at_col < rank1), v, 0.0)

    scale = float(blk) / jnp.sqrt(square_sum(live_start) + EPS)
    tr[...] = jnp.transpose(st[...])
    state[...] = masked(tr[my_rows, :], rank1, rank0) * scale
    part[...] = jnp.zeros((8, 128), F32)
    load_l.wait()
    load_r.wait()

    gath_view = lambda c, yy: gath.at[rows(c * NY + yy, slim)]
    all_view = lambda c, yy: state_all.at[rows(c * NY + yy, slim)]
    sum_view = lambda c, yy: part_all.at[c * NY + yy]

    def collect():
        state_all[my_rows, :] = state[...].astype(BF)
        part_all[slot] = part[...]
        sums = spread_out(sum_view, sum_ss, sum_rs)
        full = spread_out(all_view, all_ss, all_rs)
        pass_on(sum_view, sums, sum_ss, sum_rs)
        pass_on(all_view, full, all_ss, all_rs)
        rest(sums)
        rest(full)
        total = part_all[0]
        for i in range(1, 2 * NY):
            total = total + part_all[i]
        sent(sums)
        sent(full)
        return total

    def overall(total, scale):
        for line in range(1, ITERS + 1):
            s = total[line : line + 1, 0:1]
            scale = scale * (float(blk) / jnp.sqrt(scale * scale * s + EPS))
        return scale

    def turn():
        total = collect()
        scale = overall(total, jnp.ones((1, 1), F32))
        pick = jnp.where(at_row + slot * slim == at_col, 1.0, 0.0).astype(BF)
        first = dot_abt(pick, state_all[...]) * scale
        near_out[...] = first.astype(BF)
        to = (lax.rem(seg + 1, nseg), term)
        step = remote(near_out, near_in, near_sem.at[0], near_sem.at[1], to)
        step.start()
        step.wait()
        near = jnp.where(seg > 0, near_in[...].astype(F32), 0.0)
        x = masked(first + 0.5 * near, rank0, rank1)
        state[...] = x
        note(0, x)

    def iteration(n, _):
        h = lax.div(n, ITERS)
        gain = env_scale[h, 0:1, 0:1]

        @pl.when(n == ITERS)
        def _():
            turn()

        x = state[...].astype(BF)

        @pl.when(h == 0)
        def _():
            gath[my_rows, :] = (dot_abt(x, env[0]) * gain).astype(BF)

        @pl.when(h == 1)
        def _():
            gath[my_rows, :] = (dot_ab(x, env[1]) * gain).astype(BF)

        out = spread_out(gath_view, gath_ss, gath_rs)
        pass_on(gath_view, out, gath_ss, gath_rs)

        def apply_first(at):
            def one(w, _):
                inner[w, at, :] = dot_abt(gath[at, :], ops[h, w]).astype(BF)
                return 0

            lax.fori_loop(0, terms, one, 0)

        apply_first(ours)
        rest(out)
        apply_first(other)

        def apply_second(at):
            acc = dot_ab(ops[1 - h, 0, at, :], inner[0])
            for w in range(1, terms):
                acc = acc + dot_ab(ops[1 - h, w, at, :], inner[w])
            return acc

        s1_out[...] = apply_second(other).astype(BF)
        pair = remote(s1_out, s1_in, s1_sem.at[0], s1_sem.at[1], buddy)
        pair.start()
        own[...] = apply_second(ours)
        sent(out)
        pair.wait_recv()
        own[...] += s1_in[...].astype(F32)
        pieces = []
        for i in range(3):
            to = lax.rem(y + 1 + i, NY)
            s2_out[i] = own[rows(to, slim), :].astype(BF)
            piece = remote(s2_out.at[i], s2_in.at[i], s2_ss.at[i], s2_rs.at[i], chip(i + 1))
            piece.start()
            pieces.append(piece)
        total = own[rows(y, slim), :]
        for i in range(3):
            pieces[i].wait_recv()
            total = total + s2_in[i].astype(F32)
        high = total.astype(BF)

        def advance(applied):
            live_row = jnp.where(h == 0, rank1, rank0)
            live_col = jnp.where(h == 0, rank0, rank1)
            x = masked(2.0 * state[...] - applied * gain, live_row, live_col)
            state[...] = x
            note(1 + n - h * ITERS, x)

        @pl.when(h == 0)
        def _():
            advance(dot_ab(high, env[0]))

        @pl.when(h == 1)
        def _():
            advance(dot_abt(high, env[1]))

        pair.wait_send()
        for piece in pieces:
            piece.wait_send()
        return 0

    lax.fori_loop(0, 2 * ITERS, iteration, 0)
    total = collect()
    scale = overall(total, float(blk) / jnp.sqrt(total[0:1, 0:1] + EPS))
    out_ref[...] = state_all[...].astype(F32) * scale


def per_device(nseg, left_blocks, right_blocks, start_state, left_transfer, right_transfer, ranks):
    blk, terms = left_blocks.shape[-1], left_blocks.shape[1]
    levels = nseg.bit_length() - 1
    half, wide, slim = blk // 2, blk // NY, blk // (2 * NY)
    dma = pltpu.SemaphoreType.DMA
    scratch = [
        pltpu.VMEM((2, terms, blk, blk), BF),
        pltpu.VMEM((blk, blk), F32),
        pltpu.VMEM((blk, blk), F32),
        pltpu.VMEM((blk, blk), BF),
        pltpu.VMEM((levels + 1, wide, blk), BF),
        pltpu.VMEM((levels, blk, blk), BF),
        pltpu.VMEM((2, blk, blk), BF),
        pltpu.VMEM((2, 8, 128), F32),
        pltpu.VMEM((blk, blk), BF),
        pltpu.VMEM((terms, blk, blk), BF),
        pltpu.VMEM((half, blk), F32),
        pltpu.VMEM((half, blk), BF),
        pltpu.VMEM((half, blk), BF),
        pltpu.VMEM((3, slim, blk), BF),
        pltpu.VMEM((3, slim, blk), BF),
        pltpu.VMEM((slim, blk), F32),
        pltpu.VMEM((8, 128), F32),
        pltpu.VMEM((blk, blk), BF),
        pltpu.VMEM((2 * NY, 8, 128), F32),
        pltpu.VMEM((slim, blk), BF),
        pltpu.VMEM((slim, blk), BF),
        dma((4,)),
        dma((levels + 1,)), dma((levels + 1,)),
        dma((levels, 3)), dma((levels, 3)),
        dma((7,)), dma((7,)),
        dma((7,)), dma((7,)),
        dma((7,)), dma((7,)),
        dma((7,)), dma((7,)),
        dma((2,)),
        dma((3,)), dma((3,)),
        dma((2,)),
    ]
    any_space = pl.BlockSpec(memory_space=pl.ANY)
    final = pl.pallas_call(
        functools.partial(kernel, nseg, blk, terms),
        out_shape=jax.ShapeDtypeStruct((blk, blk), F32),
        in_specs=[any_space] * 5 + [pl.BlockSpec(memory_space=pltpu.SMEM)],
        out_specs=pl.BlockSpec(memory_space=pltpu.VMEM),
        scratch_shapes=scratch,
        compiler_params=pltpu.CompilerParams(
            collective_id=0, has_side_effects=True, vmem_limit_bytes=48 * 1024 * 1024
        ),
        name="dmrg",
    )(left_blocks, right_blocks, start_state, left_transfer, right_transfer, ranks)
    return final[None]


def solution(mesh):
    in_specs = (
        P("seg", "term", None, None),
        P("seg", "term", None, None),
        P("seg", None, None),
        P("seg", None, None),
        P("seg", None, None),
        P("seg", None),
    )
    out_specs = P("seg", None, None)
    return jax.shard_map(
        functools.partial(per_device, mesh.shape["seg"]),
        mesh=mesh, in_specs=in_specs, out_specs=out_specs, check_vma=False,
    )
```

```python
import functools

import jax
import jax.numpy as jnp
from jax import lax
from jax.experimental import pallas as pl
from jax.experimental.pallas import tpu as pltpu
from jax.sharding import PartitionSpec as P

MESH = pl.DeviceIdType.MESH
BF = jnp.bfloat16
F32 = jnp.float32
EPS = 1e-06
ITERS = 2
NY = 4


def dot_ab(a, b):
    return jnp.dot(a, b, preferred_element_type=F32)


def dot_abt(a, b):
    return lax.dot_general(a, b, (((1,), (1,)), ((), ())), preferred_element_type=F32)


def kernel(
    nseg, blk, terms,
    left_hbm, right_hbm, start_hbm, lt_hbm, rt_hbm, ranks_hbm, out_ref,
    ops, ranks, tr, st, unit, hop, link, win, env, env_scale, norms, gath, inner, own, s1_out, s1_in, s2_out, s2_in,
    state, part, state_all, part_all, near_out, near_in,
    in_sem, hop_ss, hop_rs, win_ss, win_rs, norm_ss, norm_rs, early_ss, early_rs, env_ss, env_rs, gath_ss, gath_rs, all_ss, all_rs, sum_ss, sum_rs,
    s1_sem, s2_ss, s2_rs, near_sem,
):
    seg, term = lax.axis_index("seg"), lax.axis_index("term")
    y, core = lax.div(term, 2), lax.rem(term, 2)
    sign = 1 - 2 * core
    place = jnp.where(core == 0, seg, nseg - 1 - seg)
    half, wide, slim = blk // 2, blk // NY, blk // (2 * NY)
    buddy = (seg, term + sign)

    def along(by):
        return (lax.rem(seg + sign * by + nseg, nseg), term)

    def chip(by):
        return (seg, lax.rem(y + by, NY) * 2 + core)

    def rows(index, size):
        return pl.ds(pl.multiple_of(index * size, size), size)

    def remote(src, dst, ss, rs, to):
        return pltpu.make_async_remote_copy(
            src_ref=src, dst_ref=dst, send_sem=ss, recv_sem=rs, device_id=to, device_id_type=MESH
        )

    load_l = pltpu.make_async_copy(left_hbm.at[0], ops.at[0], in_sem.at[0])
    load_r = pltpu.make_async_copy(right_hbm.at[0], ops.at[1], in_sem.at[1])
    load_s = pltpu.make_async_copy(start_hbm.at[0], st, in_sem.at[2])
    load_lt = pltpu.make_async_copy(lt_hbm.at[0], tr, in_sem.at[3])
    load_rt = pltpu.make_async_copy(rt_hbm.at[0], tr, in_sem.at[3])

    @pl.when(core == 0)
    def _():
        load_lt.start()

    @pl.when(core == 1)
    def _():
        load_rt.start()

    load_k = pltpu.make_async_copy(ranks_hbm, ranks, in_sem.at[4])
    load_k.start()
    load_s.start()
    load_l.start()
    load_r.start()

    barrier = pltpu.get_barrier_semaphore()
    sources = [chip(1), chip(2), chip(3), buddy, along(-1), along(-4), along(-8), (lax.rem(seg + nseg - 1, nseg), term)]
    for to in sources:
        pl.semaphore_signal(barrier, inc=1, device_id=to, device_id_type=MESH)
    load_lt.wait()

    root = float(blk) ** 0.5
    at_row = lax.broadcasted_iota(jnp.int32, (slim, blk), 0)
    at_col = lax.broadcasted_iota(jnp.int32, (slim, blk), 1)

    def set_unit(i, _):
        unit[rows(i, slim), :] = tr[rows(i, slim), :].astype(BF)
        return 0

    lax.fori_loop(0, 2 * NY, set_unit, 0)
    pl.semaphore_wait(barrier, len(sources))

    slot = core * NY + y
    my_rows = rows(slot, slim)
    other = rows(1 - core, half)
    ours = rows(core, half)

    def masked(x, low, high):
        live = (at_row + slot * slim < low) & (at_col < high)
        return jnp.where(live, x, 0.0)

    def note(line, x):
        part[pl.ds(line, 1), :] = jnp.broadcast_to(jnp.sum(x * x, axis=(0, 1), keepdims=True), (1, 128))

    def set_start():
        load_s.wait()
        load_k.wait()
        rank0, rank1 = ranks[0, 0], ranks[0, 1]

        def one(i, acc):
            v = st[rows(i, slim), :]
            v = jnp.where((at_row + i * slim < rank0) & (at_col < rank1), v, 0.0)
            st[rows(i, slim), :] = v
            return acc + jnp.sum((v * v).reshape(slim // 8, 8, blk), axis=0)

        acc = lax.fori_loop(0, 2 * NY, one, jnp.zeros((8, blk), F32))
        scale = float(blk) / jnp.sqrt(jnp.sum(acc, axis=(0, 1), keepdims=True) + EPS)
        tr[...] = jnp.transpose(st[...] * scale)
        unit[...] = tr[...].astype(BF)
        state[...] = tr[my_rows, :]
        part[...] = jnp.zeros((8, 128), F32)

    mine = rows(y, wide)

    def gated(distance, x):
        return jnp.where(place < distance, 0.0, x)

    def send_on(j, p, src, by):
        step = remote(src, hop.at[j, p], hop_ss.at[j, p], hop_rs.at[j, p], along(by))
        step.start()
        return step

    def times(j, p, right, distance):
        a = hop[j, p]
        return gated(distance, a.astype(F32) + dot_ab(a, right))

    def my_half(p):
        return rows(2 * y + p, slim)

    steps = [send_on(0, p, unit.at[my_half(p)], 1) for p in range(2)]
    for j in range(3):
        for p in range(2):
            steps[2 * j + p].wait_recv()
            x = (tr[my_half(p), :] + times(j, p, unit[...], 1)).astype(BF)
            if j < 2:
                link[j, p] = x
                steps.append(send_on(j + 1, p, link.at[j, p], 1))
            else:
                win[0, my_half(p), :] = x
    for step in steps:
        step.wait_send()

    for k in range(2):
        w = win.at[k]
        spread = [
            remote(w.at[mine], w.at[mine], win_ss.at[k, i], win_rs.at[k, i], chip(i + 1)) for i in range(3)
        ]
        for i in (1, 0, 2):
            spread[i].start()
        steps = [send_on(3 + k, p, w.at[my_half(p)], 4 << k) for p in range(2)]
        if k == 0:
            set_start()
            base = w[mine, :].astype(F32)
            for i in (None, 0, 2, 1):
                if i is None:
                    for step in steps:
                        step.wait_recv()
                    yy = y
                    acc = jnp.concatenate([hop[3, 0], hop[3, 1]], axis=0).astype(F32)
                else:
                    spread[i].wait_recv()
                    yy = lax.rem(y + NY - 1 - i, NY)
                left = jnp.concatenate([hop[3, p, :, rows(yy, wide)] for p in range(2)], axis=0)
                acc = acc + dot_ab(left, win[k, rows(yy, wide), :])
            win[1, mine, :] = (base + gated(4, acc)).astype(BF)
            for sp in steps:
                sp.wait_send()
        else:
            for i in (0, 2, 1):
                spread[i].wait_recv()
        for sp in spread:
            sp.wait_send()

    for j in range(nseg // 8 - 1):
        by, slot_on = (8, 5 + j) if j < nseg // 8 - 2 else (1, 5 + j)
        for p in range(2):
            steps[2 * j + p].wait_recv()
            x = win[1, my_half(p), :].astype(F32) + times(4 + j, p, win[1], 8)
            link[2 + j, p] = x.astype(BF)
            steps.append(send_on(slot_on, p, link.at[2 + j, p], by))
    for step in steps[-2:]:
        step.wait_recv()
    for step in steps:
        step.wait_send()
    came = jnp.concatenate([hop[3 + nseg // 8, p] for p in range(2)], axis=0)
    at_wide = lax.broadcasted_iota(jnp.int32, (wide, blk), 0) + y * wide
    eye_rows = jnp.where(at_wide == lax.broadcasted_iota(jnp.int32, (wide, blk), 1), 1.0, 0.0)
    rows_f = eye_rows + gated(1, came.astype(F32))
    env[core, mine, :] = rows_f.astype(BF)
    peak = jnp.maximum(jnp.max(jnp.abs(rows_f), axis=(0, 1), keepdims=True), 1e-30)
    scaled = rows_f / peak
    squares = jnp.sum(scaled * scaled, axis=(0, 1), keepdims=True)
    norms[core, y, 0] = jnp.broadcast_to(peak, (8, 128))
    norms[core, y, 1] = jnp.broadcast_to(squares, (8, 128))

    def spread_out(view, ss, rs):
        own_view = view(core, y)
        out = [remote(own_view, own_view, ss.at[i], rs.at[i], chip(i + 1)) for i in range(3)]
        out.append(remote(own_view, own_view, ss.at[3], rs.at[3], buddy))
        for o in out:
            o.start()
        return out

    def pass_on(view, out, ss, rs):
        for i in (0, 2, 1):
            got = view(core, lax.rem(y + NY - 1 - i, NY))
            out[i].wait_recv()
            fwd = remote(got, got, ss.at[4 + i], rs.at[4 + i], buddy)
            fwd.start()
            out.append(fwd)

    def rest(out):
        for o in out[3:]:
            o.wait_recv()

    def sent(out):
        for o in out:
            o.wait_send()

    rank0, rank1 = ranks[0, 0], ranks[0, 1]
    gath_view = lambda c, yy: gath.at[rows(c * NY + yy, slim)]
    all_view = lambda c, yy: state_all.at[rows(c * NY + yy, slim)]
    sum_view = lambda c, yy: part_all.at[c * NY + yy]

    def collect():
        state_all[my_rows, :] = state[...].astype(BF)
        part_all[slot] = part[...]
        sums = spread_out(sum_view, sum_ss, sum_rs)
        full = spread_out(all_view, all_ss, all_rs)
        pass_on(sum_view, sums, sum_ss, sum_rs)
        pass_on(all_view, full, all_ss, all_rs)
        rest(sums)
        rest(full)
        total = part_all[0]
        for i in range(1, 2 * NY):
            total = total + part_all[i]
        sent(sums)
        sent(full)
        return total

    def overall(total, scale):
        for line in range(1, ITERS + 1):
            s = total[line : line + 1, 0:1]
            scale = scale * (float(blk) / jnp.sqrt(scale * scale * s + EPS))
        return scale

    def turn():
        @pl.when(core == 0)
        def _():
            env_from_buddy()

        total = collect()
        scale = overall(total, jnp.ones((1, 1), F32))
        pick = jnp.where(at_row + slot * slim == at_col, 1.0, 0.0).astype(BF)
        first = dot_abt(pick, state_all[...]) * scale
        near_out[...] = first.astype(BF)
        to = (lax.rem(seg + 1, nseg), term)
        step = remote(near_out, near_in, near_sem.at[0], near_sem.at[1], to)
        step.start()
        step.wait()
        near = jnp.where(seg > 0, near_in[...].astype(F32), 0.0)
        x = masked(first + 0.5 * near, rank0, rank1)
        state[...] = x
        note(0, x)

    def apply_first(at, h, gain):
        for w in range(terms):
            inner[w, at, :] = (dot_abt(gath[at, :], ops[h, w]) * gain).astype(BF)

    def apply_second(at, h):
        acc = dot_ab(ops[1 - h, 0, at, :], inner[0])
        for w in range(1, terms):
            acc = acc + dot_ab(ops[1 - h, w, at, :], inner[w])
        return acc

    def add_up(h, out, late):
        s1_out[...] = apply_second(other, h).astype(BF)
        pair = remote(s1_out, s1_in, s1_sem.at[0], s1_sem.at[1], buddy)
        pair.start()
        own[...] = apply_second(ours, h)
        sent(out)
        pair.wait_recv()
        pieces = [None] * 3
        for i in (1, 0, 2):
            to = rows(lax.rem(y + 1 + i, NY), slim)
            s2_out[i] = (own[to, :] + s1_in[to, :].astype(F32)).astype(BF)
            pieces[i] = remote(s2_out.at[i], s2_in.at[i], s2_ss.at[i], s2_rs.at[i], chip(i + 1))
            pieces[i].start()
        total = own[rows(y, slim), :] + s1_in[rows(y, slim), :].astype(F32)
        late()
        for i in (0, 2, 1):
            pieces[i].wait_recv()
            total = total + s2_in[i].astype(F32)
        pair.wait_send()
        for piece in pieces:
            piece.wait_send()
        return total.astype(BF)

    def advance(line, applied, gain, live_row, live_col):
        x = masked(2.0 * state[...] - applied * gain, live_row, live_col)
        state[...] = x
        note(line, x)

    cols = lambda yy: gath.at[:, rows(yy, wide)]
    norm_view = lambda c, yy: norms.at[c, yy]
    env_view = lambda c, yy: env.at[c, rows(yy, wide)]

    def early(i):
        block = cols(y) if i < 4 else cols(lax.rem(y + NY - 1 - (i - 4), NY))
        to = chip(i + 1) if i < 3 else buddy
        return remote(block, block, early_ss.at[i], early_rs.at[i], to)

    def env_copy(i):
        block = env_view(core, y if i < 4 else lax.rem(y + NY - 1 - (i - 4), NY))
        return remote(block, block, env_ss.at[i], env_rs.at[i], chip(i + 1) if i < 3 else buddy)

    def env_pass_on():
        for i in (0, 2, 1):
            env_copy(i).wait_recv()
            env_copy(4 + i).start()

    def env_from_buddy():
        for i in range(3, 7):
            block = env_view(1 - core, y if i < 4 else lax.rem(y + NY - 1 - (i - 4), NY))
            remote(block, block, env_ss.at[i], env_rs.at[i], buddy).wait_recv()

    def spread_env():
        @pl.when(core == 0)
        def _():
            env_pass_on()

        @pl.when(core == 1)
        def _():
            for i in range(4):
                env_copy(i).start()

    @pl.when(core == 0)
    def _():
        gath[:, mine] = dot_abt(unit[...], env[0, mine, :]).astype(BF)
        for i in range(4):
            early(i).start()
        for i in range(4):
            env_copy(i).start()

    norm_out = spread_out(norm_view, norm_ss, norm_rs)
    pass_on(norm_view, norm_out, norm_ss, norm_rs)

    @pl.when(core == 0)
    def _():
        for i in (0, 2, 1):
            come = cols(lax.rem(y + NY - 1 - i, NY))
            remote(come, come, early_ss.at[i], early_rs.at[i], chip(i + 1)).wait_recv()
            early(4 + i).start()

    rest(norm_out)
    for h in range(2):
        peaks = [norms[h, i, 0, 0:1, 0:1] for i in range(NY)]
        top = functools.reduce(jnp.maximum, peaks)
        whole = jnp.zeros((1, 1), F32)
        for i in range(NY):
            ratio = peaks[i] / top
            whole = whole + norms[h, i, 1, 0:1, 0:1] * (ratio * ratio)
        env_scale[h] = jnp.broadcast_to(root / (top * jnp.sqrt(whole + EPS)), (8, 128))

    @pl.when(core == 1)
    def _():
        for i in range(3, 7):
            come = cols(y) if i < 4 else cols(lax.rem(y + NY - 1 - (i - 4), NY))
            remote(come, come, early_ss.at[i], early_rs.at[i], buddy).wait_recv()

    load_l.wait()
    gain = env_scale[0, 0:1, 0:1]
    apply_first(ours, 0, gain)
    apply_first(other, 0, gain)

    @pl.when(core == 0)
    def _():
        for i in range(7):
            early(i).wait_send()

    load_r.wait()
    total = add_up(0, norm_out, spread_env)

    @pl.when(core == 1)
    def _():
        env_from_buddy()

    advance(1, dot_ab(total, env[0]), gain, rank1, rank0)

    def iteration(n, _):
        h = lax.div(n, ITERS)
        gain = env_scale[h, 0:1, 0:1]

        @pl.when(n == ITERS)
        def _():
            turn()

        x = state[...].astype(BF)

        @pl.when(h == 0)
        def _():
            gath[my_rows, :] = (dot_abt(x, env[0]) * gain).astype(BF)

        @pl.when(h == 1)
        def _():
            gath[my_rows, :] = (dot_ab(x, env[1]) * gain).astype(BF)

        out = spread_out(gath_view, gath_ss, gath_rs)
        pass_on(gath_view, out, gath_ss, gath_rs)
        apply_first(ours, h, 1.0)
        rest(out)
        apply_first(other, h, 1.0)
        total = add_up(h, out, lambda: None)

        @pl.when(h == 0)
        def _():
            advance(1 + n, dot_ab(total, env[0]), gain, rank1, rank0)

            @pl.when(core == 1)
            def _():
                env_pass_on()

        @pl.when(h == 1)
        def _():
            advance(1 + n - ITERS, dot_abt(total, env[1]), gain, rank0, rank1)

        return 0

    lax.fori_loop(1, 2 * ITERS, iteration, 0)
    for i in range(7):
        env_copy(i).wait_send()
    total = collect()
    scale = overall(total, float(blk) / jnp.sqrt(total[0:1, 0:1] + EPS))
    out_ref[...] = state_all[...].astype(F32) * scale


def per_device(nseg, left_blocks, right_blocks, start_state, left_transfer, right_transfer, ranks):
    blk, terms = left_blocks.shape[-1], left_blocks.shape[1]
    half, wide, slim = blk // 2, blk // NY, blk // (2 * NY)
    dma = pltpu.SemaphoreType.DMA
    scratch = [
        pltpu.VMEM((2, terms, blk, blk), BF),
        pltpu.SMEM((1, 2), jnp.int32),
        pltpu.VMEM((blk, blk), F32),
        pltpu.VMEM((blk, blk), F32),
        pltpu.VMEM((blk, blk), BF),
        pltpu.VMEM((4 + nseg // 8, 2, slim, blk), BF),
        pltpu.VMEM((1 + nseg // 8, 2, slim, blk), BF),
        pltpu.VMEM((2, blk, blk), BF),
        pltpu.VMEM((2, blk, blk), BF),
        pltpu.VMEM((2, 8, 128), F32),
        pltpu.VMEM((2, NY, 2, 8, 128), F32),
        pltpu.VMEM((blk, blk), BF),
        pltpu.VMEM((terms, blk, blk), BF),
        pltpu.VMEM((half, blk), F32),
        pltpu.VMEM((half, blk), BF),
        pltpu.VMEM((half, blk), BF),
        pltpu.VMEM((3, slim, blk), BF),
        pltpu.VMEM((3, slim, blk), BF),
        pltpu.VMEM((slim, blk), F32),
        pltpu.VMEM((8, 128), F32),
        pltpu.VMEM((blk, blk), BF),
        pltpu.VMEM((2 * NY, 8, 128), F32),
        pltpu.VMEM((slim, blk), BF),
        pltpu.VMEM((slim, blk), BF),
        dma((5,)),
        dma((4 + nseg // 8, 2)), dma((4 + nseg // 8, 2)),
        dma((2, 3)), dma((2, 3)),
        dma((7,)), dma((7,)),
        dma((7,)), dma((7,)),
        dma((7,)), dma((7,)),
        dma((7,)), dma((7,)),
        dma((7,)), dma((7,)),
        dma((7,)), dma((7,)),
        dma((2,)),
        dma((3,)), dma((3,)),
        dma((2,)),
    ]
    hbm = pl.BlockSpec(memory_space=pltpu.HBM)
    final = pl.pallas_call(
        functools.partial(kernel, nseg, blk, terms),
        out_shape=jax.ShapeDtypeStruct((blk, blk), F32),
        in_specs=[hbm] * 6,
        out_specs=pl.BlockSpec(memory_space=pltpu.VMEM),
        scratch_shapes=scratch,
        compiler_params=pltpu.CompilerParams(
            collective_id=0, has_side_effects=True, vmem_limit_bytes=52 * 1024 * 1024
        ),
        name="dmrg",
    )(left_blocks, right_blocks, start_state, left_transfer, right_transfer, ranks)
    return final[None]


def solution(mesh):
    in_specs = (
        P("seg", "term", None, None),
        P("seg", "term", None, None),
        P("seg", None, None),
        P("seg", None, None),
        P("seg", None, None),
        P("seg", None),
    )
    out_specs = P("seg", None, None)
    return jax.shard_map(
        functools.partial(per_device, mesh.shape["seg"]),
        mesh=mesh, in_specs=in_specs, out_specs=out_specs, check_vma=False,
    )
```

```python
import functools

import jax
import jax.numpy as jnp
from jax import lax
from jax.experimental import pallas as pl
from jax.experimental.pallas import tpu as pltpu
from jax.sharding import PartitionSpec as P

MESH = pl.DeviceIdType.MESH
BF = jnp.bfloat16
F32 = jnp.float32
EPS = 1e-06
ITERS = 2
NY = 4


def dot_ab(a, b):
    return jnp.dot(a, b, preferred_element_type=F32)


def dot_abt(a, b):
    return lax.dot_general(a, b, (((1,), (1,)), ((), ())), preferred_element_type=F32)


def kernel(
    nseg, blk, terms,
    left_hbm, right_hbm, start_hbm, lt_hbm, rt_hbm, ranks_hbm, out_ref,
    ops, ranks, tr, st, unit, hop, link, win, env, env_scale, norms, gath, inner, own, s1_out, s1_in, s2_out, s2_in,
    state, part, state_all, part_all, turned, swap_out, swap_in, placing,
    in_sem, hop_ss, hop_rs, win_ss, win_rs, norm_ss, norm_rs, early_ss, early_rs, env_ss, env_rs, gath_ss, gath_rs, all_ss, all_rs, sum_ss, sum_rs,
    s1_sem, s2_ss, s2_rs, swap_ss, swap_rs,
):
    seg, term = lax.axis_index("seg"), lax.axis_index("term")
    y, core = lax.div(term, 2), lax.rem(term, 2)
    sign = 1 - 2 * core
    place = jnp.where(core == 0, seg, nseg - 1 - seg)
    half, wide, slim = blk // 2, blk // NY, blk // (2 * NY)
    buddy = (seg, term + sign)

    def along(by):
        return (lax.rem(seg + sign * by + nseg, nseg), term)

    def chip(by):
        return (seg, lax.rem(y + by, NY) * 2 + core)

    def rows(index, size):
        return pl.ds(pl.multiple_of(index * size, size), size)

    def remote(src, dst, ss, rs, to):
        return pltpu.make_async_remote_copy(
            src_ref=src, dst_ref=dst, send_sem=ss, recv_sem=rs, device_id=to, device_id_type=MESH
        )

    load_l = pltpu.make_async_copy(left_hbm.at[0], ops.at[0], in_sem.at[0])
    load_r = pltpu.make_async_copy(right_hbm.at[0], ops.at[1], in_sem.at[1])
    load_s = pltpu.make_async_copy(start_hbm.at[0], st, in_sem.at[2])
    load_lt = pltpu.make_async_copy(lt_hbm.at[0], tr, in_sem.at[3])
    load_rt = pltpu.make_async_copy(rt_hbm.at[0], tr, in_sem.at[3])

    @pl.when(core == 0)
    def _():
        load_lt.start()

    @pl.when(core == 1)
    def _():
        load_rt.start()

    load_k = pltpu.make_async_copy(ranks_hbm, ranks, in_sem.at[4])
    load_k.start()
    load_s.start()
    load_l.start()
    load_r.start()

    barrier = pltpu.get_barrier_semaphore()
    sources = [chip(1), chip(2), chip(3), buddy, along(-1), along(-4), along(-8)]
    for to in sources:
        pl.semaphore_signal(barrier, inc=1, device_id=to, device_id_type=MESH)
    load_lt.wait()

    root = float(blk) ** 0.5
    at_row = lax.broadcasted_iota(jnp.int32, (slim, blk), 0)
    at_col = lax.broadcasted_iota(jnp.int32, (slim, blk), 1)

    def set_unit(i, _):
        unit[rows(i, slim), :] = tr[rows(i, slim), :].astype(BF)
        return 0

    lax.fori_loop(0, 2 * NY, set_unit, 0)
    pl.semaphore_wait(barrier, len(sources))

    slot = core * NY + y
    my_rows = rows(slot, slim)
    other = rows(1 - core, half)
    ours = rows(core, half)

    def masked(x, low, high):
        live = (at_row + slot * slim < low) & (at_col < high)
        return jnp.where(live, x, 0.0)

    def note(line, x):
        part[pl.ds(line, 1), :] = jnp.broadcast_to(jnp.sum(x * x, axis=(0, 1), keepdims=True), (1, 128))

    def set_start():
        load_s.wait()
        load_k.wait()
        rank0, rank1 = ranks[0, 0], ranks[0, 1]

        def one(i, acc):
            v = st[rows(i, slim), :]
            v = jnp.where((at_row + i * slim < rank0) & (at_col < rank1), v, 0.0)
            st[rows(i, slim), :] = v
            return acc + jnp.sum((v * v).reshape(slim // 8, 8, blk), axis=0)

        acc = lax.fori_loop(0, 2 * NY, one, jnp.zeros((8, blk), F32))
        scale = float(blk) / jnp.sqrt(jnp.sum(acc, axis=(0, 1), keepdims=True) + EPS)
        tr[...] = jnp.transpose(st[...] * scale)
        unit[...] = tr[...].astype(BF)
        state[...] = tr[my_rows, :]
        part[...] = jnp.zeros((8, 128), F32)
        turned[...] = jnp.zeros_like(turned)
        for q in range(2 * NY):
            at = lax.broadcasted_iota(jnp.int32, (2 * slim, blk), 0)
            to = lax.broadcasted_iota(jnp.int32, (2 * slim, blk), 1) - q * slim
            placing[q * 2 * slim : (q + 1) * 2 * slim, :] = jnp.where((at == to) & (at < slim), 1.0, 0.0).astype(BF)

    mine = rows(y, wide)

    def gated(distance, x):
        return jnp.where(place < distance, 0.0, x)

    def send_on(j, p, src, by):
        step = remote(src, hop.at[j, p], hop_ss.at[j, p], hop_rs.at[j, p], along(by))
        step.start()
        return step

    def times(j, p, right, distance):
        a = hop[j, p]
        return gated(distance, a.astype(F32) + dot_ab(a, right))

    def my_half(p):
        return rows(2 * y + p, slim)

    steps = [send_on(0, p, unit.at[my_half(p)], 1) for p in range(2)]
    for j in range(3):
        for p in range(2):
            steps[2 * j + p].wait_recv()
            x = (tr[my_half(p), :] + times(j, p, unit[...], 1)).astype(BF)
            if j < 2:
                link[j, p] = x
                steps.append(send_on(j + 1, p, link.at[j, p], 1))
            else:
                win[0, my_half(p), :] = x
    for step in steps:
        step.wait_send()

    for k in range(2):
        w = win.at[k]
        spread = [
            remote(w.at[mine], w.at[mine], win_ss.at[k, i], win_rs.at[k, i], chip(i + 1)) for i in range(3)
        ]
        for i in (1, 0, 2):
            spread[i].start()
        steps = [send_on(3 + k, p, w.at[my_half(p)], 4 << k) for p in range(2)]
        if k == 0:
            set_start()
            base = w[mine, :].astype(F32)
            for i in (None, 0, 2, 1):
                if i is None:
                    for step in steps:
                        step.wait_recv()
                    yy = y
                    acc = jnp.concatenate([hop[3, 0], hop[3, 1]], axis=0).astype(F32)
                else:
                    spread[i].wait_recv()
                    yy = lax.rem(y + NY - 1 - i, NY)
                left = jnp.concatenate([hop[3, p, :, rows(yy, wide)] for p in range(2)], axis=0)
                acc = acc + dot_ab(left, win[k, rows(yy, wide), :])
            win[1, mine, :] = (base + gated(4, acc)).astype(BF)
            for sp in steps:
                sp.wait_send()
        else:
            for i in (0, 2, 1):
                spread[i].wait_recv()
        for sp in spread:
            sp.wait_send()

    for j in range(nseg // 8 - 1):
        by, slot_on = (8, 5 + j) if j < nseg // 8 - 2 else (1, 5 + j)
        for p in range(2):
            steps[2 * j + p].wait_recv()
            x = win[1, my_half(p), :].astype(F32) + times(4 + j, p, win[1], 8)
            link[2 + j, p] = x.astype(BF)
            steps.append(send_on(slot_on, p, link.at[2 + j, p], by))
    for step in steps[-2:]:
        step.wait_recv()
    for step in steps:
        step.wait_send()
    came = jnp.concatenate([hop[3 + nseg // 8, p] for p in range(2)], axis=0)
    at_wide = lax.broadcasted_iota(jnp.int32, (wide, blk), 0) + y * wide
    eye_rows = jnp.where(at_wide == lax.broadcasted_iota(jnp.int32, (wide, blk), 1), 1.0, 0.0)
    rows_f = eye_rows + gated(1, came.astype(F32))
    env[core, mine, :] = rows_f.astype(BF)
    peak = jnp.maximum(jnp.max(jnp.abs(rows_f), axis=(0, 1), keepdims=True), 1e-30)
    scaled = rows_f / peak
    squares = jnp.sum(scaled * scaled, axis=(0, 1), keepdims=True)
    norms[core, y, 0] = jnp.broadcast_to(peak, (8, 128))
    norms[core, y, 1] = jnp.broadcast_to(squares, (8, 128))

    def spread_out(view, ss, rs):
        own_view = view(core, y)
        out = [remote(own_view, own_view, ss.at[i], rs.at[i], chip(i + 1)) for i in range(3)]
        out.append(remote(own_view, own_view, ss.at[3], rs.at[3], buddy))
        for o in out:
            o.start()
        return out

    def pass_on(view, out, ss, rs):
        for i in (0, 2, 1):
            got = view(core, lax.rem(y + NY - 1 - i, NY))
            out[i].wait_recv()
            fwd = remote(got, got, ss.at[4 + i], rs.at[4 + i], buddy)
            fwd.start()
            out.append(fwd)

    def rest(out):
        for o in out[3:]:
            o.wait_recv()

    def sent(out):
        for o in out:
            o.wait_send()

    rank0, rank1 = ranks[0, 0], ranks[0, 1]
    gath_view = lambda c, yy: gath.at[rows(c * NY + yy, slim)]
    all_view = lambda c, yy: state_all.at[rows(c * NY + yy, slim)]
    sum_view = lambda c, yy: part_all.at[c * NY + yy]

    def collect():
        state_all[my_rows, :] = state[...].astype(BF)
        part_all[slot] = part[...]
        sums = spread_out(sum_view, sum_ss, sum_rs)
        full = spread_out(all_view, all_ss, all_rs)
        pass_on(sum_view, sums, sum_ss, sum_rs)
        pass_on(all_view, full, all_ss, all_rs)
        rest(sums)
        rest(full)
        total = part_all[0]
        for i in range(1, 2 * NY):
            total = total + part_all[i]
        sent(sums)
        sent(full)
        return total

    def overall(total, scale):
        for line in range(1, ITERS + 1):
            s = total[line : line + 1, 0:1]
            scale = scale * (float(blk) / jnp.sqrt(scale * scale * s + EPS))
        return scale

    def turn():
        @pl.when(core == 0)
        def _():
            env_from_buddy()

        turned[0:slim, :] = state[...]
        for line in range(1, ITERS + 1):
            v = part[line : line + 1, 0:1]
            high = v.astype(BF).astype(F32)
            mid = (v - high).astype(BF).astype(F32)
            for j, piece in enumerate((high, mid, v - high - mid)):
                at = slim + 3 * (line - 1) + j
                turned[at : at + 1, :] = jnp.broadcast_to(piece, (1, blk))
        swap_out[...] = jnp.transpose(turned[...]).astype(BF)
        copies = []
        for there in (1, 0):
            for i in range(2 * NY):
                dy, dc = i // 2, i % 2
                if there or i:
                    to_y, to_core = lax.rem(y + dy, NY), core if dc == 0 else 1 - core
                    to = (lax.rem(seg + there, nseg), to_y * 2 + to_core)
                    at = 2 * NY * there + i
                    copy = remote(
                        swap_out.at[rows(to_core * NY + to_y, slim)], swap_in.at[there, slot],
                        swap_ss.at[at], swap_rs.at[at], to,
                    )
                    copy.start()
                    copies.append(copy)
        swap_in[0, slot] = swap_out[my_rows, :]
        for copy in copies:
            copy.wait_recv()
        wide_rows = [jnp.concatenate([swap_in[g, q] for q in range(2 * NY)], axis=1) for g in range(2)]
        both = dot_ab(jnp.concatenate(wide_rows, axis=0), placing[...])
        lane = lax.broadcasted_iota(jnp.int32, (1, 2 * slim), 1)

        def seen(g):
            sums = swap_in[g, 0, 0:16, :].astype(F32)
            for q in range(1, 2 * NY):
                sums = sums + swap_in[g, q, 0:16, :].astype(F32)
            scale = jnp.ones((1, 1), F32)
            for line in range(1, ITERS + 1):
                at = slim + 3 * (line - 1)
                s = jnp.sum(jnp.where((lane >= at) & (lane < at + 3), sums[0:1, :], 0.0), axis=(0, 1), keepdims=True)
                scale = scale * (float(blk) / jnp.sqrt(scale * scale * s + EPS))
            return both[g * slim : (g + 1) * slim] * scale

        near = jnp.where(seg > 0, seen(1).astype(BF).astype(F32), 0.0)
        x = masked(seen(0) + 0.5 * near, rank0, rank1)
        state[...] = x
        note(0, x)
        for copy in copies:
            copy.wait_send()

    def apply_first(at, h, gain):
        for w in range(terms):
            inner[w, at, :] = (dot_abt(gath[at, :], ops[h, w]) * gain).astype(BF)

    def apply_second(at, h):
        acc = dot_ab(ops[1 - h, 0, at, :], inner[0])
        for w in range(1, terms):
            acc = acc + dot_ab(ops[1 - h, w, at, :], inner[w])
        return acc

    def add_up(h, out, late):
        s1_out[...] = apply_second(other, h).astype(BF)
        pair = remote(s1_out, s1_in, s1_sem.at[0], s1_sem.at[1], buddy)
        pair.start()
        own[...] = apply_second(ours, h)
        sent(out)
        pair.wait_recv()
        pieces = [None] * 3
        for i in (1, 0, 2):
            to = rows(lax.rem(y + 1 + i, NY), slim)
            s2_out[i] = (own[to, :] + s1_in[to, :].astype(F32)).astype(BF)
            pieces[i] = remote(s2_out.at[i], s2_in.at[i], s2_ss.at[i], s2_rs.at[i], chip(i + 1))
            pieces[i].start()
        total = own[rows(y, slim), :] + s1_in[rows(y, slim), :].astype(F32)
        late()
        for i in (0, 2, 1):
            pieces[i].wait_recv()
            total = total + s2_in[i].astype(F32)
        pair.wait_send()
        for piece in pieces:
            piece.wait_send()
        return total.astype(BF)

    def advance(line, applied, gain, live_row, live_col):
        x = masked(2.0 * state[...] - applied * gain, live_row, live_col)
        state[...] = x
        note(line, x)

    cols = lambda yy: gath.at[:, rows(yy, wide)]
    norm_view = lambda c, yy: norms.at[c, yy]
    env_view = lambda c, yy: env.at[c, rows(yy, wide)]

    def early(i):
        block = cols(y) if i < 4 else cols(lax.rem(y + NY - 1 - (i - 4), NY))
        to = chip(i + 1) if i < 3 else buddy
        return remote(block, block, early_ss.at[i], early_rs.at[i], to)

    def env_copy(i):
        block = env_view(core, y if i < 4 else lax.rem(y + NY - 1 - (i - 4), NY))
        return remote(block, block, env_ss.at[i], env_rs.at[i], chip(i + 1) if i < 3 else buddy)

    def env_pass_on():
        for i in (0, 2, 1):
            env_copy(i).wait_recv()
            env_copy(4 + i).start()

    def env_from_buddy():
        for i in range(3, 7):
            block = env_view(1 - core, y if i < 4 else lax.rem(y + NY - 1 - (i - 4), NY))
            remote(block, block, env_ss.at[i], env_rs.at[i], buddy).wait_recv()

    def spread_env():
        @pl.when(core == 0)
        def _():
            env_pass_on()

        @pl.when(core == 1)
        def _():
            for i in range(4):
                env_copy(i).start()

    @pl.when(core == 0)
    def _():
        gath[:, mine] = dot_abt(unit[...], env[0, mine, :]).astype(BF)
        for i in range(4):
            early(i).start()
        for i in range(4):
            env_copy(i).start()

    norm_out = spread_out(norm_view, norm_ss, norm_rs)
    pass_on(norm_view, norm_out, norm_ss, norm_rs)

    @pl.when(core == 0)
    def _():
        for i in (0, 2, 1):
            come = cols(lax.rem(y + NY - 1 - i, NY))
            remote(come, come, early_ss.at[i], early_rs.at[i], chip(i + 1)).wait_recv()
            early(4 + i).start()

    rest(norm_out)
    for h in range(2):
        peaks = [norms[h, i, 0, 0:1, 0:1] for i in range(NY)]
        top = functools.reduce(jnp.maximum, peaks)
        whole = jnp.zeros((1, 1), F32)
        for i in range(NY):
            ratio = peaks[i] / top
            whole = whole + norms[h, i, 1, 0:1, 0:1] * (ratio * ratio)
        env_scale[h] = jnp.broadcast_to(root / (top * jnp.sqrt(whole + EPS)), (8, 128))

    @pl.when(core == 1)
    def _():
        for i in range(3, 7):
            come = cols(y) if i < 4 else cols(lax.rem(y + NY - 1 - (i - 4), NY))
            remote(come, come, early_ss.at[i], early_rs.at[i], buddy).wait_recv()

    load_l.wait()
    gain = env_scale[0, 0:1, 0:1]
    apply_first(ours, 0, gain)
    apply_first(other, 0, gain)

    @pl.when(core == 0)
    def _():
        for i in range(7):
            early(i).wait_send()

    load_r.wait()
    total = add_up(0, norm_out, spread_env)

    @pl.when(core == 1)
    def _():
        env_from_buddy()

    advance(1, dot_ab(total, env[0]), gain, rank1, rank0)

    def iteration(n, _):
        h = lax.div(n, ITERS)
        gain = env_scale[h, 0:1, 0:1]

        @pl.when(n == ITERS)
        def _():
            turn()

        x = state[...].astype(BF)

        @pl.when(h == 0)
        def _():
            gath[my_rows, :] = (dot_abt(x, env[0]) * gain).astype(BF)

        @pl.when(h == 1)
        def _():
            gath[my_rows, :] = (dot_ab(x, env[1]) * gain).astype(BF)

        out = spread_out(gath_view, gath_ss, gath_rs)
        pass_on(gath_view, out, gath_ss, gath_rs)
        apply_first(ours, h, 1.0)
        rest(out)
        apply_first(other, h, 1.0)
        total = add_up(h, out, lambda: None)

        @pl.when(h == 0)
        def _():
            advance(1 + n, dot_ab(total, env[0]), gain, rank1, rank0)

            @pl.when(core == 1)
            def _():
                env_pass_on()

        @pl.when(h == 1)
        def _():
            advance(1 + n - ITERS, dot_abt(total, env[1]), gain, rank0, rank1)

        return 0

    lax.fori_loop(1, 2 * ITERS, iteration, 0)
    for i in range(7):
        env_copy(i).wait_send()
    total = collect()
    scale = overall(total, float(blk) / jnp.sqrt(total[0:1, 0:1] + EPS))
    out_ref[...] = state_all[...].astype(F32) * scale


def per_device(nseg, left_blocks, right_blocks, start_state, left_transfer, right_transfer, ranks):
    blk, terms = left_blocks.shape[-1], left_blocks.shape[1]
    half, wide, slim = blk // 2, blk // NY, blk // (2 * NY)
    dma = pltpu.SemaphoreType.DMA
    scratch = [
        pltpu.VMEM((2, terms, blk, blk), BF),
        pltpu.SMEM((1, 2), jnp.int32),
        pltpu.VMEM((blk, blk), F32),
        pltpu.VMEM((blk, blk), F32),
        pltpu.VMEM((blk, blk), BF),
        pltpu.VMEM((4 + nseg // 8, 2, slim, blk), BF),
        pltpu.VMEM((1 + nseg // 8, 2, slim, blk), BF),
        pltpu.VMEM((2, blk, blk), BF),
        pltpu.VMEM((2, blk, blk), BF),
        pltpu.VMEM((2, 8, 128), F32),
        pltpu.VMEM((2, NY, 2, 8, 128), F32),
        pltpu.VMEM((blk, blk), BF),
        pltpu.VMEM((terms, blk, blk), BF),
        pltpu.VMEM((half, blk), F32),
        pltpu.VMEM((half, blk), BF),
        pltpu.VMEM((half, blk), BF),
        pltpu.VMEM((3, slim, blk), BF),
        pltpu.VMEM((3, slim, blk), BF),
        pltpu.VMEM((slim, blk), F32),
        pltpu.VMEM((8, 128), F32),
        pltpu.VMEM((blk, blk), BF),
        pltpu.VMEM((2 * NY, 8, 128), F32),
        pltpu.VMEM((2 * slim, blk), F32),
        pltpu.VMEM((blk, 2 * slim), BF),
        pltpu.VMEM((2, 2 * NY, slim, 2 * slim), BF),
        pltpu.VMEM((2 * blk, blk), BF),
        dma((5,)),
        dma((4 + nseg // 8, 2)), dma((4 + nseg // 8, 2)),
        dma((2, 3)), dma((2, 3)),
        dma((7,)), dma((7,)),
        dma((7,)), dma((7,)),
        dma((7,)), dma((7,)),
        dma((7,)), dma((7,)),
        dma((7,)), dma((7,)),
        dma((7,)), dma((7,)),
        dma((2,)),
        dma((3,)), dma((3,)),
        dma((4 * NY,)), dma((4 * NY,)),
    ]
    hbm = pl.BlockSpec(memory_space=pltpu.HBM)
    final = pl.pallas_call(
        functools.partial(kernel, nseg, blk, terms),
        out_shape=jax.ShapeDtypeStruct((blk, blk), F32),
        in_specs=[hbm] * 6,
        out_specs=pl.BlockSpec(memory_space=pltpu.VMEM),
        scratch_shapes=scratch,
        compiler_params=pltpu.CompilerParams(
            collective_id=0, has_side_effects=True, vmem_limit_bytes=52 * 1024 * 1024
        ),
        name="dmrg",
    )(left_blocks, right_blocks, start_state, left_transfer, right_transfer, ranks)
    return final[None]


def solution(mesh):
    in_specs = (
        P("seg", "term", None, None),
        P("seg", "term", None, None),
        P("seg", None, None),
        P("seg", None, None),
        P("seg", None, None),
        P("seg", None),
    )
    out_specs = P("seg", None, None)
    return jax.shard_map(
        functools.partial(per_device, mesh.shape["seg"]),
        mesh=mesh, in_specs=in_specs, out_specs=out_specs, check_vma=False,
    )
```

```python
import functools

import jax
import jax.numpy as jnp
from jax import lax
from jax.experimental import pallas as pl
from jax.experimental.pallas import tpu as pltpu
from jax.sharding import PartitionSpec as P

MESH = pl.DeviceIdType.MESH
BF = jnp.bfloat16
F32 = jnp.float32
EPS = 1e-06
ITERS = 2
NY = 4
PIECES = 4


def dot_ab(a, b):
    return jnp.dot(a, b, preferred_element_type=F32)


def dot_abt(a, b):
    return lax.dot_general(a, b, (((1,), (1,)), ((), ())), preferred_element_type=F32)


def kernel(
    nseg, blk, terms,
    left_hbm, right_hbm, start_hbm, lt_hbm, rt_hbm, ranks_hbm, out_ref,
    ops, ranks, tr, st, unit, hop, link, win, env, env_scale, norms, gath, inner, own, s1_out, s1_in, s2_out, s2_in,
    state, part, state_all, part_all, turned, swap_out, swap_in, placing,
    in_sem, hop_ss, hop_rs, win_ss, win_rs, norm_ss, norm_rs, early_ss, early_rs, env_ss, env_rs, gath_ss, gath_rs, all_ss, all_rs, sum_ss, sum_rs,
    s1_sem, s2_ss, s2_rs, swap_ss, swap_rs,
):
    seg, term = lax.axis_index("seg"), lax.axis_index("term")
    y, core = lax.div(term, 2), lax.rem(term, 2)
    sign = 1 - 2 * core
    place = jnp.where(core == 0, seg, nseg - 1 - seg)
    half, wide, slim = blk // 2, blk // NY, blk // (2 * NY)
    buddy = (seg, term + sign)

    def along(by):
        return (lax.rem(seg + sign * by + nseg, nseg), term)

    def chip(by):
        return (seg, lax.rem(y + by, NY) * 2 + core)

    def rows(index, size):
        return pl.ds(pl.multiple_of(index * size, size), size)

    def remote(src, dst, ss, rs, to):
        return pltpu.make_async_remote_copy(
            src_ref=src, dst_ref=dst, send_sem=ss, recv_sem=rs, device_id=to, device_id_type=MESH
        )

    load_l = pltpu.make_async_copy(left_hbm.at[0], ops.at[0], in_sem.at[0])
    load_r = pltpu.make_async_copy(right_hbm.at[0], ops.at[1], in_sem.at[1])
    load_s = pltpu.make_async_copy(start_hbm.at[0], st, in_sem.at[2])
    load_lt = pltpu.make_async_copy(lt_hbm.at[0], tr, in_sem.at[3])
    load_rt = pltpu.make_async_copy(rt_hbm.at[0], tr, in_sem.at[3])

    @pl.when(core == 0)
    def _():
        load_lt.start()

    @pl.when(core == 1)
    def _():
        load_rt.start()

    barrier = pltpu.get_barrier_semaphore()
    sources = [chip(1), chip(2), chip(3), buddy, along(-1), along(-4), along(-8)]
    for to in sources:
        pl.semaphore_signal(barrier, inc=1, device_id=to, device_id_type=MESH)

    load_k = pltpu.make_async_copy(ranks_hbm, ranks, in_sem.at[4])
    load_k.start()
    load_s.start()
    load_l.start()
    load_r.start()

    load_lt.wait()

    root = float(blk) ** 0.5
    at_row = lax.broadcasted_iota(jnp.int32, (slim, blk), 0)
    at_col = lax.broadcasted_iota(jnp.int32, (slim, blk), 1)

    def set_unit(i, _):
        unit[rows(i, slim), :] = tr[rows(i, slim), :].astype(BF)
        return 0

    lax.fori_loop(0, 2 * NY, set_unit, 0)
    pl.semaphore_wait(barrier, len(sources))

    slot = core * NY + y
    my_rows = rows(slot, slim)
    other = rows(1 - core, half)
    ours = rows(core, half)

    def masked(x, low, high):
        live = (at_row + slot * slim < low) & (at_col < high)
        return jnp.where(live, x, 0.0)

    def note(line, x):
        part[pl.ds(line, 1), :] = jnp.broadcast_to(jnp.sum(x * x, axis=(0, 1), keepdims=True), (1, 128))

    def set_start():
        load_s.wait()
        load_k.wait()
        rank0, rank1 = ranks[0, 0], ranks[0, 1]

        def one(i, acc):
            v = st[rows(i, slim), :]
            v = jnp.where((at_row + i * slim < rank0) & (at_col < rank1), v, 0.0)
            st[rows(i, slim), :] = v
            return acc + jnp.sum((v * v).reshape(slim // 8, 8, blk), axis=0)

        acc = lax.fori_loop(0, 2 * NY, one, jnp.zeros((8, blk), F32))
        scale = float(blk) / jnp.sqrt(jnp.sum(acc, axis=(0, 1), keepdims=True) + EPS)
        tr[...] = jnp.transpose(st[...] * scale)
        unit[...] = tr[...].astype(BF)
        state[...] = tr[my_rows, :]
        part[...] = jnp.zeros((8, 128), F32)
        turned[...] = jnp.zeros_like(turned)
        for q in range(2 * NY):
            at = lax.broadcasted_iota(jnp.int32, (2 * slim, blk), 0)
            to = lax.broadcasted_iota(jnp.int32, (2 * slim, blk), 1) - q * slim
            placing[q * 2 * slim : (q + 1) * 2 * slim, :] = jnp.where((at == to) & (at < slim), 1.0, 0.0).astype(BF)

    mine = rows(y, wide)

    def gated(distance, x):
        return jnp.where(place < distance, 0.0, x)

    def send_on(j, p, src, by):
        step = remote(src, hop.at[j, p], hop_ss.at[j, p], hop_rs.at[j, p], along(by))
        step.start()
        return step

    def times(j, p, right, distance):
        a = hop[j, p]
        return gated(distance, a.astype(F32) + dot_ab(a, right))

    def my_piece(p):
        return rows(PIECES * y + p, wide // PIECES)

    steps = [send_on(0, p, unit.at[my_piece(p)], 1) for p in range(PIECES)]
    for j in range(3):
        for p in range(PIECES):
            steps[PIECES * j + p].wait_recv()
            x = (tr[my_piece(p), :] + times(j, p, unit[...], 1)).astype(BF)
            if j < 2:
                link[j, p] = x
                steps.append(send_on(j + 1, p, link.at[j, p], 1))
            else:
                win[0, my_piece(p), :] = x
    for step in steps:
        step.wait_send()

    for k in range(2):
        w = win.at[k]
        spread = [
            remote(w.at[mine], w.at[mine], win_ss.at[k, i], win_rs.at[k, i], chip(i + 1)) for i in range(3)
        ]
        for i in (1, 0, 2):
            spread[i].start()
        steps = [send_on(3 + k, p, w.at[my_piece(p)], 4 << k) for p in range(PIECES)]
        if k == 0:
            set_start()
            base = w[mine, :].astype(F32)
            for i in (None, 0, 2, 1):
                if i is None:
                    for step in steps:
                        step.wait_recv()
                    yy = y
                    acc = jnp.concatenate([hop[3, p] for p in range(PIECES)], axis=0).astype(F32)
                else:
                    spread[i].wait_recv()
                    yy = lax.rem(y + NY - 1 - i, NY)
                left = jnp.concatenate([hop[3, p, :, rows(yy, wide)] for p in range(PIECES)], axis=0)
                acc = acc + dot_ab(left, win[k, rows(yy, wide), :])
            win[1, mine, :] = (base + gated(4, acc)).astype(BF)
            for sp in steps:
                sp.wait_send()
        else:
            for i in (0, 2, 1):
                spread[i].wait_recv()
        for sp in spread:
            sp.wait_send()

    for j in range(nseg // 8 - 1):
        by, slot_on = (8, 5 + j) if j < nseg // 8 - 2 else (1, 5 + j)
        for p in range(PIECES):
            steps[PIECES * j + p].wait_recv()
            x = win[1, my_piece(p), :].astype(F32) + times(4 + j, p, win[1], 8)
            link[2 + j, p] = x.astype(BF)
            steps.append(send_on(slot_on, p, link.at[2 + j, p], by))
    for step in steps[-PIECES:]:
        step.wait_recv()
    for step in steps:
        step.wait_send()
    came = jnp.concatenate([hop[3 + nseg // 8, p] for p in range(PIECES)], axis=0)
    at_wide = lax.broadcasted_iota(jnp.int32, (wide, blk), 0) + y * wide
    eye_rows = jnp.where(at_wide == lax.broadcasted_iota(jnp.int32, (wide, blk), 1), 1.0, 0.0)
    rows_f = eye_rows + gated(1, came.astype(F32))
    env[core, mine, :] = rows_f.astype(BF)
    peak = jnp.maximum(jnp.max(jnp.abs(rows_f), axis=(0, 1), keepdims=True), 1e-30)
    scaled = rows_f / peak
    squares = jnp.sum(scaled * scaled, axis=(0, 1), keepdims=True)
    norms[core, y, 0] = jnp.broadcast_to(peak, (8, 128))
    norms[core, y, 1] = jnp.broadcast_to(squares, (8, 128))

    def spread_out(view, ss, rs):
        own_view = view(core, y)
        out = [remote(own_view, own_view, ss.at[i], rs.at[i], chip(i + 1)) for i in range(3)]
        out.append(remote(own_view, own_view, ss.at[3], rs.at[3], buddy))
        for o in out:
            o.start()
        return out

    def pass_on(view, out, ss, rs):
        for i in (0, 2, 1):
            got = view(core, lax.rem(y + NY - 1 - i, NY))
            out[i].wait_recv()
            fwd = remote(got, got, ss.at[4 + i], rs.at[4 + i], buddy)
            fwd.start()
            out.append(fwd)

    def rest(out):
        for o in out[3:]:
            o.wait_recv()

    def sent(out):
        for o in out:
            o.wait_send()

    rank0, rank1 = ranks[0, 0], ranks[0, 1]
    gath_view = lambda c, yy: gath.at[rows(c * NY + yy, slim)]
    all_view = lambda c, yy: state_all.at[rows(c * NY + yy, slim)]
    sum_view = lambda c, yy: part_all.at[c * NY + yy]

    def collect():
        state_all[my_rows, :] = state[...].astype(BF)
        part_all[slot] = part[...]
        sums = spread_out(sum_view, sum_ss, sum_rs)
        full = spread_out(all_view, all_ss, all_rs)
        pass_on(sum_view, sums, sum_ss, sum_rs)
        pass_on(all_view, full, all_ss, all_rs)
        rest(sums)
        rest(full)
        total = part_all[0]
        for i in range(1, 2 * NY):
            total = total + part_all[i]
        sent(sums)
        sent(full)
        return total

    def overall(total, scale):
        for line in range(1, ITERS + 1):
            s = total[line : line + 1, 0:1]
            scale = scale * (float(blk) / jnp.sqrt(scale * scale * s + EPS))
        return scale

    def turn():
        @pl.when(core == 0)
        def _():
            env_from_buddy()

        turned[0:slim, :] = state[...]
        for line in range(1, ITERS + 1):
            v = part[line : line + 1, 0:1]
            high = v.astype(BF).astype(F32)
            mid = (v - high).astype(BF).astype(F32)
            for j, piece in enumerate((high, mid, v - high - mid)):
                at = slim + 3 * (line - 1) + j
                turned[at : at + 1, :] = jnp.broadcast_to(piece, (1, blk))
        swap_out[...] = jnp.transpose(turned[...]).astype(BF)
        copies = []
        for there in (1, 0):
            for i in range(2 * NY):
                dy, dc = i // 2, i % 2
                if there or i:
                    to_y, to_core = lax.rem(y + dy, NY), core if dc == 0 else 1 - core
                    to = (lax.rem(seg + there, nseg), to_y * 2 + to_core)
                    at = 2 * NY * there + i
                    copy = remote(
                        swap_out.at[rows(to_core * NY + to_y, slim)], swap_in.at[there, slot],
                        swap_ss.at[at], swap_rs.at[at], to,
                    )
                    copy.start()
                    copies.append(copy)
        swap_in[0, slot] = swap_out[my_rows, :]
        for copy in copies:
            copy.wait_recv()
        wide_rows = [jnp.concatenate([swap_in[g, q] for q in range(2 * NY)], axis=1) for g in range(2)]
        both = dot_ab(jnp.concatenate(wide_rows, axis=0), placing[...])
        lane = lax.broadcasted_iota(jnp.int32, (1, 2 * slim), 1)

        def seen(g):
            sums = swap_in[g, 0, 0:16, :].astype(F32)
            for q in range(1, 2 * NY):
                sums = sums + swap_in[g, q, 0:16, :].astype(F32)
            scale = jnp.ones((1, 1), F32)
            for line in range(1, ITERS + 1):
                at = slim + 3 * (line - 1)
                s = jnp.sum(jnp.where((lane >= at) & (lane < at + 3), sums[0:1, :], 0.0), axis=(0, 1), keepdims=True)
                scale = scale * (float(blk) / jnp.sqrt(scale * scale * s + EPS))
            return both[g * slim : (g + 1) * slim] * scale

        near = jnp.where(seg > 0, seen(1).astype(BF).astype(F32), 0.0)
        x = masked(seen(0) + 0.5 * near, rank0, rank1)
        state[...] = x
        note(0, x)
        for copy in copies:
            copy.wait_send()

    def apply_first(at, h, gain):
        for w in range(terms):
            inner[w, at, :] = (dot_abt(gath[at, :], ops[h, w]) * gain).astype(BF)

    def apply_second(at, h):
        acc = dot_ab(ops[1 - h, 0, at, :], inner[0])
        for w in range(1, terms):
            acc = acc + dot_ab(ops[1 - h, w, at, :], inner[w])
        return acc

    def add_up(h, out, late):
        s1_out[...] = apply_second(other, h).astype(BF)
        pair = remote(s1_out, s1_in, s1_sem.at[0], s1_sem.at[1], buddy)
        pair.start()
        own[...] = apply_second(ours, h)
        sent(out)
        pair.wait_recv()
        pieces = [None] * 3
        for i in (1, 0, 2):
            to = rows(lax.rem(y + 1 + i, NY), slim)
            s2_out[i] = (own[to, :] + s1_in[to, :].astype(F32)).astype(BF)
            pieces[i] = remote(s2_out.at[i], s2_in.at[i], s2_ss.at[i], s2_rs.at[i], chip(i + 1))
            pieces[i].start()
        total = own[rows(y, slim), :] + s1_in[rows(y, slim), :].astype(F32)
        late()
        for i in (0, 2, 1):
            pieces[i].wait_recv()
            total = total + s2_in[i].astype(F32)
        pair.wait_send()
        for piece in pieces:
            piece.wait_send()
        return total.astype(BF)

    def advance(line, applied, gain, live_row, live_col):
        x = masked(2.0 * state[...] - applied * gain, live_row, live_col)
        state[...] = x
        note(line, x)

    cols = lambda yy: gath.at[:, rows(yy, wide)]
    norm_view = lambda c, yy: norms.at[c, yy]
    env_view = lambda c, yy: env.at[c, rows(yy, wide)]

    def early(i):
        block = cols(y) if i < 4 else cols(lax.rem(y + NY - 1 - (i - 4), NY))
        to = chip(i + 1) if i < 3 else buddy
        return remote(block, block, early_ss.at[i], early_rs.at[i], to)

    def env_copy(i):
        block = env_view(core, y if i < 4 else lax.rem(y + NY - 1 - (i - 4), NY))
        return remote(block, block, env_ss.at[i], env_rs.at[i], chip(i + 1) if i < 3 else buddy)

    def env_pass_on():
        for i in (0, 2, 1):
            env_copy(i).wait_recv()
            env_copy(4 + i).start()

    def env_from_buddy():
        for i in range(3, 7):
            block = env_view(1 - core, y if i < 4 else lax.rem(y + NY - 1 - (i - 4), NY))
            remote(block, block, env_ss.at[i], env_rs.at[i], buddy).wait_recv()

    def spread_env():
        @pl.when(core == 0)
        def _():
            env_pass_on()

    @pl.when(core == 0)
    def _():
        gath[:, mine] = dot_abt(unit[...], env[0, mine, :]).astype(BF)
        for i in range(4):
            early(i).start()

    norm_out = spread_out(norm_view, norm_ss, norm_rs)
    pass_on(norm_view, norm_out, norm_ss, norm_rs)

    @pl.when(core == 0)
    def _():
        for i in (0, 2, 1):
            come = cols(lax.rem(y + NY - 1 - i, NY))
            remote(come, come, early_ss.at[i], early_rs.at[i], chip(i + 1)).wait_recv()
            early(4 + i).start()
        for i in range(4):
            env_copy(i).start()

    rest(norm_out)
    for h in range(2):
        peaks = [norms[h, i, 0, 0:1, 0:1] for i in range(NY)]
        top = functools.reduce(jnp.maximum, peaks)
        whole = jnp.zeros((1, 1), F32)
        for i in range(NY):
            ratio = peaks[i] / top
            whole = whole + norms[h, i, 1, 0:1, 0:1] * (ratio * ratio)
        env_scale[h] = jnp.broadcast_to(root / (top * jnp.sqrt(whole + EPS)), (8, 128))

    @pl.when(core == 1)
    def _():
        for i in range(3, 7):
            come = cols(y) if i < 4 else cols(lax.rem(y + NY - 1 - (i - 4), NY))
            remote(come, come, early_ss.at[i], early_rs.at[i], buddy).wait_recv()

    load_l.wait()
    gain = env_scale[0, 0:1, 0:1]
    apply_first(ours, 0, gain)
    apply_first(other, 0, gain)

    @pl.when(core == 0)
    def _():
        for i in range(7):
            early(i).wait_send()

    load_r.wait()
    total = add_up(0, norm_out, spread_env)

    @pl.when(core == 1)
    def _():
        env_from_buddy()

    advance(1, dot_ab(total, env[0]), gain, rank1, rank0)

    def iteration(n, _):
        h = lax.div(n, ITERS)
        gain = env_scale[h, 0:1, 0:1]

        @pl.when(n == ITERS)
        def _():
            turn()

        x = state[...].astype(BF)

        @pl.when(h == 0)
        def _():
            gath[my_rows, :] = (dot_abt(x, env[0]) * gain).astype(BF)

        @pl.when(h == 1)
        def _():
            gath[my_rows, :] = (dot_ab(x, env[1]) * gain).astype(BF)

        out = spread_out(gath_view, gath_ss, gath_rs)
        pass_on(gath_view, out, gath_ss, gath_rs)

        @pl.when((n == 1) & (core == 1))
        def _():
            for i in range(4):
                env_copy(i).start()

        apply_first(ours, h, 1.0)
        rest(out)
        apply_first(other, h, 1.0)
        total = add_up(h, out, lambda: None)

        @pl.when(h == 0)
        def _():
            advance(1 + n, dot_ab(total, env[0]), gain, rank1, rank0)

            @pl.when(core == 1)
            def _():
                env_pass_on()

        @pl.when(h == 1)
        def _():
            advance(1 + n - ITERS, dot_abt(total, env[1]), gain, rank0, rank1)

        return 0

    lax.fori_loop(1, 2 * ITERS, iteration, 0)
    for i in range(7):
        env_copy(i).wait_send()
    total = collect()
    scale = overall(total, float(blk) / jnp.sqrt(total[0:1, 0:1] + EPS))
    out_ref[...] = state_all[...].astype(F32) * scale


def per_device(nseg, left_blocks, right_blocks, start_state, left_transfer, right_transfer, ranks):
    blk, terms = left_blocks.shape[-1], left_blocks.shape[1]
    half, wide, slim = blk // 2, blk // NY, blk // (2 * NY)
    dma = pltpu.SemaphoreType.DMA
    scratch = [
        pltpu.VMEM((2, terms, blk, blk), BF),
        pltpu.SMEM((1, 2), jnp.int32),
        pltpu.VMEM((blk, blk), F32),
        pltpu.VMEM((blk, blk), F32),
        pltpu.VMEM((blk, blk), BF),
        pltpu.VMEM((4 + nseg // 8, PIECES, wide // PIECES, blk), BF),
        pltpu.VMEM((1 + nseg // 8, PIECES, wide // PIECES, blk), BF),
        pltpu.VMEM((2, blk, blk), BF),
        pltpu.VMEM((2, blk, blk), BF),
        pltpu.VMEM((2, 8, 128), F32),
        pltpu.VMEM((2, NY, 2, 8, 128), F32),
        pltpu.VMEM((blk, blk), BF),
        pltpu.VMEM((terms, blk, blk), BF),
        pltpu.VMEM((half, blk), F32),
        pltpu.VMEM((half, blk), BF),
        pltpu.VMEM((half, blk), BF),
        pltpu.VMEM((3, slim, blk), BF),
        pltpu.VMEM((3, slim, blk), BF),
        pltpu.VMEM((slim, blk), F32),
        pltpu.VMEM((8, 128), F32),
        pltpu.VMEM((blk, blk), BF),
        pltpu.VMEM((2 * NY, 8, 128), F32),
        pltpu.VMEM((2 * slim, blk), F32),
        pltpu.VMEM((blk, 2 * slim), BF),
        pltpu.VMEM((2, 2 * NY, slim, 2 * slim), BF),
        pltpu.VMEM((2 * blk, blk), BF),
        dma((5,)),
        dma((4 + nseg // 8, PIECES)), dma((4 + nseg // 8, PIECES)),
        dma((2, 3)), dma((2, 3)),
        dma((7,)), dma((7,)),
        dma((7,)), dma((7,)),
        dma((7,)), dma((7,)),
        dma((7,)), dma((7,)),
        dma((7,)), dma((7,)),
        dma((7,)), dma((7,)),
        dma((2,)),
        dma((3,)), dma((3,)),
        dma((4 * NY,)), dma((4 * NY,)),
    ]
    hbm = pl.BlockSpec(memory_space=pltpu.HBM)
    final = pl.pallas_call(
        functools.partial(kernel, nseg, blk, terms),
        out_shape=jax.ShapeDtypeStruct((blk, blk), F32),
        in_specs=[hbm] * 6,
        out_specs=pl.BlockSpec(memory_space=pltpu.VMEM),
        scratch_shapes=scratch,
        compiler_params=pltpu.CompilerParams(
            collective_id=0, has_side_effects=True, vmem_limit_bytes=52 * 1024 * 1024
        ),
        name="dmrg",
    )(left_blocks, right_blocks, start_state, left_transfer, right_transfer, ranks)
    return final[None]


def solution(mesh):
    in_specs = (
        P("seg", "term", None, None),
        P("seg", "term", None, None),
        P("seg", None, None),
        P("seg", None, None),
        P("seg", None, None),
        P("seg", None),
    )
    out_specs = P("seg", None, None)
    return jax.shard_map(
        functools.partial(per_device, mesh.shape["seg"]),
        mesh=mesh, in_specs=in_specs, out_specs=out_specs, check_vma=False,
    )
```

```python
import functools

import jax
import jax.numpy as jnp
from jax import lax
from jax.experimental import pallas as pl
from jax.experimental.pallas import tpu as pltpu
from jax.sharding import PartitionSpec as P

MESH = pl.DeviceIdType.MESH
BF = jnp.bfloat16
F32 = jnp.float32
EPS = 1e-06
ITERS = 2
NY = 4
PIECES = 4


def dot_ab(a, b):
    return jnp.dot(a, b, preferred_element_type=F32)


def dot_abt(a, b):
    return lax.dot_general(a, b, (((1,), (1,)), ((), ())), preferred_element_type=F32)


def kernel(
    nseg, blk, terms,
    left_hbm, right_hbm, start_hbm, lt_hbm, rt_hbm, ranks_hbm, out_ref,
    ops, ranks, tr, st, unit, hop, link, win, env, env_scale, norms, gath, inner, own, s1_out, s1_in, s2_out, s2_in,
    state, part, state_all, part_all, turned, swap_out, swap_in, placing,
    in_sem, hop_ss, hop_rs, win_ss, win_rs, norm_ss, norm_rs, early_ss, early_rs, env_ss, env_rs, gath_ss, gath_rs, all_ss, all_rs, sum_ss, sum_rs,
    s1_sem, s2_ss, s2_rs, swap_ss, swap_rs, go,
):
    seg, term = lax.axis_index("seg"), lax.axis_index("term")
    y, core = lax.div(term, 2), lax.rem(term, 2)
    sign = 1 - 2 * core
    place = jnp.where(core == 0, seg, nseg - 1 - seg)
    half, wide, slim = blk // 2, blk // NY, blk // (2 * NY)
    buddy = (seg, term + sign)

    def along(by):
        return (lax.rem(seg + sign * by + nseg, nseg), term)

    def chip(by):
        return (seg, lax.rem(y + by, NY) * 2 + core)

    def rows(index, size):
        return pl.ds(pl.multiple_of(index * size, size), size)

    def remote(src, dst, ss, rs, to):
        return pltpu.make_async_remote_copy(
            src_ref=src, dst_ref=dst, send_sem=ss, recv_sem=rs, device_id=to, device_id_type=MESH
        )

    load_l = pltpu.make_async_copy(left_hbm.at[0], ops.at[0], in_sem.at[0])
    load_r = pltpu.make_async_copy(right_hbm.at[0], ops.at[1], in_sem.at[1])
    load_s = pltpu.make_async_copy(start_hbm.at[0], st, in_sem.at[2])
    load_lt = pltpu.make_async_copy(lt_hbm.at[0], tr, in_sem.at[3])
    load_rt = pltpu.make_async_copy(rt_hbm.at[0], tr, in_sem.at[3])

    @pl.when(core == 0)
    def _():
        load_lt.start()

    @pl.when(core == 1)
    def _():
        load_rt.start()

    barrier = pltpu.get_barrier_semaphore()
    sources = [chip(1), chip(2), chip(3), buddy, along(-1), along(-4), along(-8)]
    for to in sources:
        pl.semaphore_signal(barrier, inc=1, device_id=to, device_id_type=MESH)

    load_k = pltpu.make_async_copy(ranks_hbm, ranks, in_sem.at[4])

    load_lt.wait()
    for load in (load_k, load_s, load_l, load_r):
        load.start()

    root = float(blk) ** 0.5
    at_row = lax.broadcasted_iota(jnp.int32, (slim, blk), 0)
    at_col = lax.broadcasted_iota(jnp.int32, (slim, blk), 1)

    def set_unit(i, _):
        unit[rows(i, slim), :] = tr[rows(i, slim), :].astype(BF)
        return 0

    pl.semaphore_wait(barrier, len(sources))

    slot = core * NY + y
    my_rows = rows(slot, slim)
    other = rows(1 - core, half)
    ours = rows(core, half)

    def masked(x, low, high):
        live = (at_row + slot * slim < low) & (at_col < high)
        return jnp.where(live, x, 0.0)

    def note(line, x):
        part[pl.ds(line, 1), :] = jnp.broadcast_to(jnp.sum(x * x, axis=(0, 1), keepdims=True), (1, 128))

    def set_start():
        load_s.wait()
        load_k.wait()
        rank0, rank1 = ranks[0, 0], ranks[0, 1]

        def one(i, acc):
            v = st[rows(i, slim), :]
            v = jnp.where((at_row + i * slim < rank0) & (at_col < rank1), v, 0.0)
            st[rows(i, slim), :] = v
            return acc + jnp.sum((v * v).reshape(slim // 8, 8, blk), axis=0)

        acc = lax.fori_loop(0, 2 * NY, one, jnp.zeros((8, blk), F32))
        scale = float(blk) / jnp.sqrt(jnp.sum(acc, axis=(0, 1), keepdims=True) + EPS)
        tr[...] = jnp.transpose(st[...] * scale)
        unit[...] = tr[...].astype(BF)
        state[...] = tr[my_rows, :]
        part[...] = jnp.zeros((8, 128), F32)
        turned[...] = jnp.zeros_like(turned)
        for q in range(2 * NY):
            at = lax.broadcasted_iota(jnp.int32, (2 * slim, blk), 0)
            to = lax.broadcasted_iota(jnp.int32, (2 * slim, blk), 1) - q * slim
            placing[q * 2 * slim : (q + 1) * 2 * slim, :] = jnp.where((at == to) & (at < slim), 1.0, 0.0).astype(BF)

    mine = rows(y, wide)

    def gated(distance, x):
        return jnp.where(place < distance, 0.0, x)

    def send_on(j, p, src, by):
        step = remote(src, hop.at[j, p], hop_ss.at[j, p], hop_rs.at[j, p], along(by))
        step.start()
        return step

    def times(j, p, right, distance):
        a = hop[j, p]
        return gated(distance, a.astype(F32) + dot_ab(a, right))

    def my_piece(p):
        return rows(PIECES * y + p, wide // PIECES)

    for p in range(PIECES):
        link[0, p] = tr[my_piece(p), :].astype(BF)
    steps = [send_on(0, p, link.at[0, p], 1) for p in range(PIECES)]
    lax.fori_loop(0, 2 * NY, set_unit, 0)
    for j in range(3):
        for p in range(PIECES):
            steps[PIECES * j + p].wait_recv()
            x = (tr[my_piece(p), :] + times(j, p, unit[...], 1)).astype(BF)
            if j < 2:
                link[1 + j, p] = x
                steps.append(send_on(j + 1, p, link.at[1 + j, p], 1))
            else:
                win[0, my_piece(p), :] = x
    for step in steps:
        step.wait_send()

    def let_go():
        @pl.when(core == 0)
        def _():
            pl.semaphore_signal(go, inc=1, device_id=buddy, device_id_type=MESH)

    for k in range(2):
        w = win.at[k]

        spread = [
            remote(w.at[mine], w.at[mine], win_ss.at[k, i], win_rs.at[k, i], chip(i + 1)) for i in range(3)
        ]
        for i in (1, 0, 2):
            spread[i].start()
        steps = [send_on(3 + k, p, w.at[my_piece(p)], 4 << k) for p in range(PIECES)]
        if k == 0:
            set_start()
            base = w[mine, :].astype(F32)
            for i in (None, 0, 2, 1):
                if i is None:
                    for step in steps:
                        step.wait_recv()
                    yy = y
                    acc = jnp.concatenate([hop[3, p] for p in range(PIECES)], axis=0).astype(F32)
                else:
                    spread[i].wait_recv()
                    yy = lax.rem(y + NY - 1 - i, NY)
                left = jnp.concatenate([hop[3, p, :, rows(yy, wide)] for p in range(PIECES)], axis=0)
                acc = acc + dot_ab(left, win[k, rows(yy, wide), :])
            win[1, mine, :] = (base + gated(4, acc)).astype(BF)
            for sp in steps:
                sp.wait_send()
        else:
            for i in (0, 2, 1):
                spread[i].wait_recv()
        for sp in spread:
            sp.wait_send()

    for j in range(nseg // 8 - 1):
        by, slot_on = (8, 5 + j) if j < nseg // 8 - 2 else (1, 5 + j)
        for p in range(PIECES):
            steps[PIECES * j + p].wait_recv()
            x = win[1, my_piece(p), :].astype(F32) + times(4 + j, p, win[1], 8)
            link[3 + j, p] = x.astype(BF)
            steps.append(send_on(slot_on, p, link.at[3 + j, p], by))
    for step in steps[-PIECES:]:
        step.wait_recv()
    for step in steps:
        step.wait_send()
    came = jnp.concatenate([hop[3 + nseg // 8, p] for p in range(PIECES)], axis=0)
    at_wide = lax.broadcasted_iota(jnp.int32, (wide, blk), 0) + y * wide
    eye_rows = jnp.where(at_wide == lax.broadcasted_iota(jnp.int32, (wide, blk), 1), 1.0, 0.0)
    rows_f = eye_rows + gated(1, came.astype(F32))
    env[core, mine, :] = rows_f.astype(BF)
    peak = jnp.maximum(jnp.max(jnp.abs(rows_f), axis=(0, 1), keepdims=True), 1e-30)
    scaled = rows_f / peak
    squares = jnp.sum(scaled * scaled, axis=(0, 1), keepdims=True)
    norms[core, y, 0] = jnp.broadcast_to(peak, (8, 128))
    norms[core, y, 1] = jnp.broadcast_to(squares, (8, 128))

    def spread_out(view, ss, rs):
        own_view = view(core, y)
        out = [remote(own_view, own_view, ss.at[i], rs.at[i], chip(i + 1)) for i in range(3)]
        out.append(remote(own_view, own_view, ss.at[3], rs.at[3], buddy))
        for i in (1, 0, 2, 3):
            out[i].start()
        return out

    def pass_on(view, out, ss, rs):
        for i in (0, 2, 1):
            got = view(core, lax.rem(y + NY - 1 - i, NY))
            out[i].wait_recv()
            fwd = remote(got, got, ss.at[4 + i], rs.at[4 + i], buddy)
            fwd.start()
            out.append(fwd)

    def rest(out):
        for o in out[3:]:
            o.wait_recv()

    def sent(out):
        for o in out:
            o.wait_send()

    rank0, rank1 = ranks[0, 0], ranks[0, 1]
    gath_view = lambda c, yy: gath.at[rows(c * NY + yy, slim)]
    all_view = lambda c, yy: state_all.at[rows(c * NY + yy, slim)]
    sum_view = lambda c, yy: part_all.at[c * NY + yy]

    def collect():
        state_all[my_rows, :] = state[...].astype(BF)
        part_all[slot] = part[...]
        full = spread_out(all_view, all_ss, all_rs)
        sums = spread_out(sum_view, sum_ss, sum_rs)
        pass_on(all_view, full, all_ss, all_rs)
        pass_on(sum_view, sums, sum_ss, sum_rs)
        rest(sums)
        rest(full)
        total = part_all[0]
        for i in range(1, 2 * NY):
            total = total + part_all[i]
        sent(sums)
        sent(full)
        return total

    def overall(total, scale):
        for line in range(1, ITERS + 1):
            s = total[line : line + 1, 0:1]
            scale = scale * (float(blk) / jnp.sqrt(scale * scale * s + EPS))
        return scale

    def turn():
        @pl.when(core == 0)
        def _():
            env_arrive()
            norm_arrive()

        set_scale(1)

        turned[0:slim, :] = state[...]
        for line in range(1, ITERS + 1):
            v = part[line : line + 1, 0:1]
            high = v.astype(BF).astype(F32)
            mid = (v - high).astype(BF).astype(F32)
            for j, piece in enumerate((high, mid, v - high - mid)):
                at = slim + 3 * (line - 1) + j
                turned[at : at + 1, :] = jnp.broadcast_to(piece, (1, blk))
        swap_out[...] = jnp.transpose(turned[...]).astype(BF)
        copies = []
        for there in (1, 0):
            for i in range(2 * NY):
                dy, dc = i // 2, i % 2
                if there or i:
                    to_y, to_core = lax.rem(y + dy, NY), core if dc == 0 else 1 - core
                    to = (lax.rem(seg + there, nseg), to_y * 2 + to_core)
                    at = 2 * NY * there + i
                    copy = remote(
                        swap_out.at[rows(to_core * NY + to_y, slim)], swap_in.at[there, slot],
                        swap_ss.at[at], swap_rs.at[at], to,
                    )
                    copy.start()
                    copies.append(copy)
        swap_in[0, slot] = swap_out[my_rows, :]
        for copy in copies:
            copy.wait_recv()
        wide_rows = [jnp.concatenate([swap_in[g, q] for q in range(2 * NY)], axis=1) for g in range(2)]
        both = dot_ab(jnp.concatenate(wide_rows, axis=0), placing[...])
        lane = lax.broadcasted_iota(jnp.int32, (1, 2 * slim), 1)

        def seen(g):
            sums = swap_in[g, 0, 0:16, :].astype(F32)
            for q in range(1, 2 * NY):
                sums = sums + swap_in[g, q, 0:16, :].astype(F32)
            scale = jnp.ones((1, 1), F32)
            for line in range(1, ITERS + 1):
                at = slim + 3 * (line - 1)
                s = jnp.sum(jnp.where((lane >= at) & (lane < at + 3), sums[0:1, :], 0.0), axis=(0, 1), keepdims=True)
                scale = scale * (float(blk) / jnp.sqrt(scale * scale * s + EPS))
            return both[g * slim : (g + 1) * slim] * scale

        near = jnp.where(seg > 0, seen(1).astype(BF).astype(F32), 0.0)
        x = masked(seen(0) + 0.5 * near, rank0, rank1)
        state[...] = x
        note(0, x)
        for copy in copies:
            copy.wait_send()

    def apply_first(at, h, gain):
        for w in range(terms):
            inner[w, at, :] = (dot_abt(gath[at, :], ops[h, w]) * gain).astype(BF)

    def apply_second(at, h):
        acc = dot_ab(ops[1 - h, 0, at, :], inner[0])
        for w in range(1, terms):
            acc = acc + dot_ab(ops[1 - h, w, at, :], inner[w])
        return acc

    def add_up(h, out, late):
        s1_out[...] = apply_second(other, h).astype(BF)
        pair = remote(s1_out, s1_in, s1_sem.at[0], s1_sem.at[1], buddy)
        pair.start()
        own[...] = apply_second(ours, h)
        sent(out)
        pair.wait_recv()
        pieces = [None] * 3
        for i in (1, 0, 2):
            to = rows(lax.rem(y + 1 + i, NY), slim)
            s2_out[i] = (own[to, :] + s1_in[to, :].astype(F32)).astype(BF)
            pieces[i] = remote(s2_out.at[i], s2_in.at[i], s2_ss.at[i], s2_rs.at[i], chip(i + 1))
            pieces[i].start()
        total = own[rows(y, slim), :] + s1_in[rows(y, slim), :].astype(F32)
        late()
        for i in (0, 2, 1):
            pieces[i].wait_recv()
            total = total + s2_in[i].astype(F32)
        pair.wait_send()
        for piece in pieces:
            piece.wait_send()
        return total.astype(BF)

    def advance(line, applied, gain, live_row, live_col):
        x = masked(2.0 * state[...] - applied * gain, live_row, live_col)
        state[...] = x
        note(line, x)

    cols = lambda yy: gath.at[:, rows(yy, wide)]
    norm_view = lambda c, yy: norms.at[c, yy]
    env_view = lambda c, yy: env.at[c, rows(yy, wide)]

    def from_this_core(view, ss, rs):
        def copy(i):
            block = view(core, y if i < 4 else lax.rem(y + NY - 1 - (i - 4), NY))
            return remote(block, block, ss.at[i], rs.at[i], chip(i + 1) if i < 3 else buddy)

        def start():
            for i in (1, 0, 2, 3):
                copy(i).start()

        def forward():
            for i in (0, 2, 1):
                copy(i).wait_recv()
                copy(4 + i).start()

        def arrive():
            for i in range(3, 7):
                block = view(1 - core, y if i < 4 else lax.rem(y + NY - 1 - (i - 4), NY))
                remote(block, block, ss.at[i], rs.at[i], buddy).wait_recv()

        def finish():
            for i in range(7):
                copy(i).wait_send()

        return start, forward, arrive, finish

    norm_start, norm_forward, norm_arrive, norm_finish = from_this_core(norm_view, norm_ss, norm_rs)
    env_start, env_forward, env_arrive, env_finish = from_this_core(env_view, env_ss, env_rs)
    col_start, col_forward, col_arrive, col_finish = from_this_core(lambda c, yy: cols(yy), early_ss, early_rs)

    def set_scale(h):
        peaks = [norms[h, i, 0, 0:1, 0:1] for i in range(NY)]
        top = functools.reduce(jnp.maximum, peaks)
        whole = jnp.zeros((1, 1), F32)
        for i in range(NY):
            ratio = peaks[i] / top
            whole = whole + norms[h, i, 1, 0:1, 0:1] * (ratio * ratio)
        env_scale[h] = jnp.broadcast_to(root / (top * jnp.sqrt(whole + EPS)), (8, 128))

    def spread_env():
        @pl.when(core == 0)
        def _():
            env_forward()

    @pl.when(core == 0)
    def _():
        gath[:, mine] = dot_abt(unit[...], env[0, mine, :]).astype(BF)
        col_start()
        norm_start()
        col_forward()
        norm_forward()
        env_start()

    @pl.when(core == 1)
    def _():
        norm_arrive()
        col_arrive()

    set_scale(0)
    load_l.wait()
    gain = env_scale[0, 0:1, 0:1]
    apply_first(ours, 0, gain)
    apply_first(other, 0, gain)

    @pl.when(core == 0)
    def _():
        col_finish()

    load_r.wait()
    total = add_up(0, [], spread_env)

    @pl.when(core == 1)
    def _():
        env_arrive()

    advance(1, dot_ab(total, env[0]), gain, rank1, rank0)

    def iteration(n, _):
        h = lax.div(n, ITERS)

        @pl.when(n == ITERS)
        def _():
            turn()

        gain = env_scale[h, 0:1, 0:1]
        x = state[...].astype(BF)

        @pl.when(h == 0)
        def _():
            gath[my_rows, :] = (dot_abt(x, env[0]) * gain).astype(BF)

        @pl.when(h == 1)
        def _():
            gath[my_rows, :] = (dot_ab(x, env[1]) * gain).astype(BF)

        out = spread_out(gath_view, gath_ss, gath_rs)
        pass_on(gath_view, out, gath_ss, gath_rs)

        @pl.when((n == 1) & (core == 1))
        def _():
            env_start()
            norm_start()

        apply_first(ours, h, 1.0)
        rest(out)
        apply_first(other, h, 1.0)
        total = add_up(h, out, lambda: None)

        @pl.when(h == 0)
        def _():
            advance(1 + n, dot_ab(total, env[0]), gain, rank1, rank0)

            @pl.when(core == 1)
            def _():
                env_forward()
                norm_forward()

        @pl.when(h == 1)
        def _():
            advance(1 + n - ITERS, dot_abt(total, env[1]), gain, rank0, rank1)

        return 0

    lax.fori_loop(1, 2 * ITERS, iteration, 0)
    env_finish()
    norm_finish()
    total = collect()
    scale = overall(total, float(blk) / jnp.sqrt(total[0:1, 0:1] + EPS))
    out_ref[...] = state_all[...].astype(F32) * scale


def per_device(nseg, left_blocks, right_blocks, start_state, left_transfer, right_transfer, ranks):
    blk, terms = left_blocks.shape[-1], left_blocks.shape[1]
    half, wide, slim = blk // 2, blk // NY, blk // (2 * NY)
    dma = pltpu.SemaphoreType.DMA
    scratch = [
        pltpu.VMEM((2, terms, blk, blk), BF),
        pltpu.SMEM((1, 2), jnp.int32),
        pltpu.VMEM((blk, blk), F32),
        pltpu.VMEM((blk, blk), F32),
        pltpu.VMEM((blk, blk), BF),
        pltpu.VMEM((4 + nseg // 8, PIECES, wide // PIECES, blk), BF),
        pltpu.VMEM((2 + nseg // 8, PIECES, wide // PIECES, blk), BF),
        pltpu.VMEM((2, blk, blk), BF),
        pltpu.VMEM((2, blk, blk), BF),
        pltpu.VMEM((2, 8, 128), F32),
        pltpu.VMEM((2, NY, 2, 8, 128), F32),
        pltpu.VMEM((blk, blk), BF),
        pltpu.VMEM((terms, blk, blk), BF),
        pltpu.VMEM((half, blk), F32),
        pltpu.VMEM((half, blk), BF),
        pltpu.VMEM((half, blk), BF),
        pltpu.VMEM((3, slim, blk), BF),
        pltpu.VMEM((3, slim, blk), BF),
        pltpu.VMEM((slim, blk), F32),
        pltpu.VMEM((8, 128), F32),
        pltpu.VMEM((blk, blk), BF),
        pltpu.VMEM((2 * NY, 8, 128), F32),
        pltpu.VMEM((2 * slim, blk), F32),
        pltpu.VMEM((blk, 2 * slim), BF),
        pltpu.VMEM((2, 2 * NY, slim, 2 * slim), BF),
        pltpu.VMEM((2 * blk, blk), BF),
        dma((5,)),
        dma((4 + nseg // 8, PIECES)), dma((4 + nseg // 8, PIECES)),
        dma((2, 3)), dma((2, 3)),
        dma((7,)), dma((7,)),
        dma((7,)), dma((7,)),
        dma((7,)), dma((7,)),
        dma((7,)), dma((7,)),
        dma((7,)), dma((7,)),
        dma((7,)), dma((7,)),
        dma((2,)),
        dma((3,)), dma((3,)),
        dma((4 * NY,)), dma((4 * NY,)),
        pltpu.SemaphoreType.REGULAR,
    ]
    hbm = pl.BlockSpec(memory_space=pltpu.HBM)
    final = pl.pallas_call(
        functools.partial(kernel, nseg, blk, terms),
        out_shape=jax.ShapeDtypeStruct((blk, blk), F32),
        in_specs=[hbm] * 6,
        out_specs=pl.BlockSpec(memory_space=pltpu.VMEM),
        scratch_shapes=scratch,
        compiler_params=pltpu.CompilerParams(
            collective_id=0, has_side_effects=True, vmem_limit_bytes=52 * 1024 * 1024
        ),
        name="dmrg",
    )(left_blocks, right_blocks, start_state, left_transfer, right_transfer, ranks)
    return final[None]


def solution(mesh):
    in_specs = (
        P("seg", "term", None, None),
        P("seg", "term", None, None),
        P("seg", None, None),
        P("seg", None, None),
        P("seg", None, None),
        P("seg", None),
    )
    out_specs = P("seg", None, None)
    return jax.shard_map(
        functools.partial(per_device, mesh.shape["seg"]),
        mesh=mesh, in_specs=in_specs, out_specs=out_specs, check_vma=False,
    )
```

```python
import functools

import jax
import jax.numpy as jnp
from jax import lax
from jax.experimental import pallas as pl
from jax.experimental.pallas import tpu as pltpu
from jax.sharding import PartitionSpec as P

MESH = pl.DeviceIdType.MESH
BF = jnp.bfloat16
F32 = jnp.float32
EPS = 1e-06
ITERS = 2
NY = 4
PIECES = 4


def dot_ab(a, b):
    return jnp.dot(a, b, preferred_element_type=F32)


def dot_abt(a, b):
    return lax.dot_general(a, b, (((1,), (1,)), ((), ())), preferred_element_type=F32)


def kernel(
    nseg, blk, terms,
    left_hbm, right_hbm, start_hbm, lt_hbm, rt_hbm, ranks_hbm, out_ref,
    ops, ranks, tr, st, unit, hop, link, win, env, env_scale, norms, gath, inner, own, s1_out, s1_in, s2_out, s2_in,
    state, part, state_all, part_all, turned, swap_out, swap_in, placing,
    in_sem, hop_ss, hop_rs, win_ss, win_rs, norm_ss, norm_rs, early_ss, early_rs, env_ss, env_rs, gath_ss, gath_rs, all_ss, all_rs, sum_ss, sum_rs,
    s1_sem, s2_ss, s2_rs, swap_ss, swap_rs, go,
):
    seg, term = lax.axis_index("seg"), lax.axis_index("term")
    y, core = lax.div(term, 2), lax.rem(term, 2)
    sign = 1 - 2 * core
    place = jnp.where(core == 0, seg, nseg - 1 - seg)
    half, wide, slim = blk // 2, blk // NY, blk // (2 * NY)
    buddy = (seg, term + sign)

    def along(by):
        return (lax.rem(seg + sign * by + nseg, nseg), term)

    def chip(by):
        return (seg, lax.rem(y + by, NY) * 2 + core)

    def rows(index, size):
        return pl.ds(pl.multiple_of(index * size, size), size)

    def remote(src, dst, ss, rs, to):
        return pltpu.make_async_remote_copy(
            src_ref=src, dst_ref=dst, send_sem=ss, recv_sem=rs, device_id=to, device_id_type=MESH
        )

    load_l = pltpu.make_async_copy(left_hbm.at[0], ops.at[0], in_sem.at[0])
    load_r = pltpu.make_async_copy(right_hbm.at[0], ops.at[1], in_sem.at[1])
    load_s = pltpu.make_async_copy(start_hbm.at[0], st, in_sem.at[2])
    load_lt = pltpu.make_async_copy(lt_hbm.at[0], tr, in_sem.at[3])
    load_rt = pltpu.make_async_copy(rt_hbm.at[0], tr, in_sem.at[3])

    @pl.when(core == 0)
    def _():
        load_lt.start()

    @pl.when(core == 1)
    def _():
        load_rt.start()

    barrier = pltpu.get_barrier_semaphore()
    sources = [chip(1), chip(2), chip(3), buddy, along(-1), along(-4), along(-8)]
    for to in sources:
        pl.semaphore_signal(barrier, inc=1, device_id=to, device_id_type=MESH)

    load_k = pltpu.make_async_copy(ranks_hbm, ranks, in_sem.at[4])

    load_lt.wait()
    for load in (load_k, load_s, load_l, load_r):
        load.start()

    root = float(blk) ** 0.5
    at_row = lax.broadcasted_iota(jnp.int32, (slim, blk), 0)
    at_col = lax.broadcasted_iota(jnp.int32, (slim, blk), 1)

    def set_unit(i, _):
        unit[rows(i, slim), :] = tr[rows(i, slim), :].astype(BF)
        return 0

    pl.semaphore_wait(barrier, len(sources))

    slot = core * NY + y
    my_rows = rows(slot, slim)
    other = rows(1 - core, half)
    ours = rows(core, half)

    def masked(x, low, high):
        live = (at_row + slot * slim < low) & (at_col < high)
        return jnp.where(live, x, 0.0)

    def note(line, x):
        part[pl.ds(line, 1), :] = jnp.broadcast_to(jnp.sum(x * x, axis=(0, 1), keepdims=True), (1, 128))

    def set_start():
        load_s.wait()
        load_k.wait()
        rank0, rank1 = ranks[0, 0], ranks[0, 1]

        def one(i, acc):
            v = st[rows(i, slim), :]
            v = jnp.where((at_row + i * slim < rank0) & (at_col < rank1), v, 0.0)
            st[rows(i, slim), :] = v
            return acc + jnp.sum((v * v).reshape(slim // 8, 8, blk), axis=0)

        acc = lax.fori_loop(0, 2 * NY, one, jnp.zeros((8, blk), F32))
        scale = float(blk) / jnp.sqrt(jnp.sum(acc, axis=(0, 1), keepdims=True) + EPS)
        tr[...] = jnp.transpose(st[...] * scale)
        unit[...] = tr[...].astype(BF)
        state[...] = tr[my_rows, :]
        part[...] = jnp.zeros((8, 128), F32)
        turned[...] = jnp.zeros_like(turned)
        for q in range(2 * NY):
            at = lax.broadcasted_iota(jnp.int32, (2 * slim, blk), 0)
            to = lax.broadcasted_iota(jnp.int32, (2 * slim, blk), 1) - q * slim
            placing[q * 2 * slim : (q + 1) * 2 * slim, :] = jnp.where((at == to) & (at < slim), 1.0, 0.0).astype(BF)

    mine = rows(y, wide)

    def gated(distance, x):
        return jnp.where(place < distance, 0.0, x)

    def send_on(j, p, src, by):
        step = remote(src, hop.at[j, p], hop_ss.at[j, p], hop_rs.at[j, p], along(by))
        step.start()
        return step

    def times(j, p, right, distance):
        a = hop[j, p]
        return gated(distance, a.astype(F32) + dot_ab(a, right))

    def my_piece(p):
        return rows(PIECES * y + p, wide // PIECES)

    for p in range(PIECES):
        link[0, p] = tr[my_piece(p), :].astype(BF)
    steps = [send_on(0, p, link.at[0, p], 1) for p in range(PIECES)]
    lax.fori_loop(0, 2 * NY, set_unit, 0)
    for j in range(3):
        for p in range(PIECES):
            steps[PIECES * j + p].wait_recv()
            x = (tr[my_piece(p), :] + times(j, p, unit[...], 1)).astype(BF)
            if j < 2:
                link[1 + j, p] = x
                steps.append(send_on(j + 1, p, link.at[1 + j, p], 1))
            else:
                win[0, my_piece(p), :] = x
    for step in steps:
        step.wait_send()

    def let_go():
        @pl.when(core == 0)
        def _():
            pl.semaphore_signal(go, inc=1, device_id=buddy, device_id_type=MESH)

    for k in range(2):
        w = win.at[k]

        spread = [
            remote(w.at[mine], w.at[mine], win_ss.at[k, i], win_rs.at[k, i], chip(i + 1)) for i in range(3)
        ]
        for i in (1, 0, 2):
            spread[i].start()
        steps = [send_on(3 + k, p, w.at[my_piece(p)], 4 << k) for p in range(PIECES)]
        if k == 0:
            set_start()
            base = w[mine, :].astype(F32)
            for i in (None, 0, 2, 1):
                if i is None:
                    for step in steps:
                        step.wait_recv()
                    yy = y
                    acc = jnp.concatenate([hop[3, p] for p in range(PIECES)], axis=0).astype(F32)
                else:
                    spread[i].wait_recv()
                    yy = lax.rem(y + NY - 1 - i, NY)
                left = jnp.concatenate([hop[3, p, :, rows(yy, wide)] for p in range(PIECES)], axis=0)
                acc = acc + dot_ab(left, win[k, rows(yy, wide), :])
            win[1, mine, :] = (base + gated(4, acc)).astype(BF)
            for sp in steps:
                sp.wait_send()
        else:
            for i in (0, 2, 1):
                spread[i].wait_recv()
        for sp in spread:
            sp.wait_send()

    for j in range(nseg // 8 - 1):
        by, slot_on = (8, 5 + j) if j < nseg // 8 - 2 else (1, 5 + j)
        for p in range(PIECES):
            steps[PIECES * j + p].wait_recv()
            x = win[1, my_piece(p), :].astype(F32) + times(4 + j, p, win[1], 8)
            link[3 + j, p] = x.astype(BF)
            steps.append(send_on(slot_on, p, link.at[3 + j, p], by))
    for step in steps[-PIECES:]:
        step.wait_recv()
    for step in steps:
        step.wait_send()
    came = jnp.concatenate([hop[3 + nseg // 8, p] for p in range(PIECES)], axis=0)
    at_wide = lax.broadcasted_iota(jnp.int32, (wide, blk), 0) + y * wide
    eye_rows = jnp.where(at_wide == lax.broadcasted_iota(jnp.int32, (wide, blk), 1), 1.0, 0.0)
    rows_f = eye_rows + gated(1, came.astype(F32))
    env[core, mine, :] = rows_f.astype(BF)
    peak = jnp.maximum(jnp.max(jnp.abs(rows_f), axis=(0, 1), keepdims=True), 1e-30)
    scaled = rows_f / peak
    squares = jnp.sum(scaled * scaled, axis=(0, 1), keepdims=True)
    norms[core, y, 0] = jnp.broadcast_to(peak, (8, 128))
    norms[core, y, 1] = jnp.broadcast_to(squares, (8, 128))

    def spread_out(view, ss, rs):
        own_view = view(core, y)
        out = [remote(own_view, own_view, ss.at[i], rs.at[i], chip(i + 1)) for i in range(3)]
        out.append(remote(own_view, own_view, ss.at[3], rs.at[3], buddy))
        for i in (1, 0, 2, 3):
            out[i].start()
        return out

    def pass_on(view, out, ss, rs):
        for i in (0, 2, 1):
            got = view(core, lax.rem(y + NY - 1 - i, NY))
            out[i].wait_recv()
            fwd = remote(got, got, ss.at[4 + i], rs.at[4 + i], buddy)
            fwd.start()
            out.append(fwd)

    def rest(out):
        for o in out[3:]:
            o.wait_recv()

    def sent(out):
        for o in out:
            o.wait_send()

    rank0, rank1 = ranks[0, 0], ranks[0, 1]
    gath_view = lambda c, yy: gath.at[rows(c * NY + yy, slim)]
    all_view = lambda c, yy: state_all.at[rows(c * NY + yy, slim)]
    sum_view = lambda c, yy: part_all.at[c * NY + yy]

    def collect():
        state_all[my_rows, :] = state[...].astype(BF)
        part_all[slot] = part[...]
        full = spread_out(all_view, all_ss, all_rs)
        sums = spread_out(sum_view, sum_ss, sum_rs)
        pass_on(all_view, full, all_ss, all_rs)
        pass_on(sum_view, sums, sum_ss, sum_rs)
        rest(sums)
        rest(full)
        total = part_all[0]
        for i in range(1, 2 * NY):
            total = total + part_all[i]
        sent(sums)
        sent(full)
        return total

    def overall(total, scale):
        for line in range(1, ITERS + 1):
            s = total[line : line + 1, 0:1]
            scale = scale * (float(blk) / jnp.sqrt(scale * scale * s + EPS))
        return scale

    def turn():

        turned[0:slim, :] = state[...]
        for line in range(1, ITERS + 1):
            v = part[line : line + 1, 0:1]
            high = v.astype(BF).astype(F32)
            mid = (v - high).astype(BF).astype(F32)
            for j, piece in enumerate((high, mid, v - high - mid)):
                at = slim + 3 * (line - 1) + j
                turned[at : at + 1, :] = jnp.broadcast_to(piece, (1, blk))
        swap_out[...] = jnp.transpose(turned[...]).astype(BF)
        copies = []
        for there in (1, 0):
            for i in range(2 * NY):
                dy, dc = i // 2, i % 2
                if there or i:
                    to_y, to_core = lax.rem(y + dy, NY), core if dc == 0 else 1 - core
                    to = (lax.rem(seg + there, nseg), to_y * 2 + to_core)
                    at = 2 * NY * there + i
                    copy = remote(
                        swap_out.at[rows(to_core * NY + to_y, slim)], swap_in.at[there, slot],
                        swap_ss.at[at], swap_rs.at[at], to,
                    )
                    copy.start()
                    copies.append(copy)
        swap_in[0, slot] = swap_out[my_rows, :]

        @pl.when(core == 0)
        def _():
            env_arrive()
            norm_arrive()

        set_scale(1)
        for copy in copies:
            copy.wait_recv()
        wide_rows = [jnp.concatenate([swap_in[g, q] for q in range(2 * NY)], axis=1) for g in range(2)]
        both = dot_ab(jnp.concatenate(wide_rows, axis=0), placing[...])
        lane = lax.broadcasted_iota(jnp.int32, (1, 2 * slim), 1)

        def seen(g):
            sums = swap_in[g, 0, 0:16, :].astype(F32)
            for q in range(1, 2 * NY):
                sums = sums + swap_in[g, q, 0:16, :].astype(F32)
            scale = jnp.ones((1, 1), F32)
            for line in range(1, ITERS + 1):
                at = slim + 3 * (line - 1)
                s = jnp.sum(jnp.where((lane >= at) & (lane < at + 3), sums[0:1, :], 0.0), axis=(0, 1), keepdims=True)
                scale = scale * (float(blk) / jnp.sqrt(scale * scale * s + EPS))
            return both[g * slim : (g + 1) * slim] * scale

        near = jnp.where(seg > 0, seen(1).astype(BF).astype(F32), 0.0)
        x = masked(seen(0) + 0.5 * near, rank0, rank1)
        state[...] = x
        note(0, x)
        for copy in copies:
            copy.wait_send()

    def apply_first(at, h, gain):
        for w in range(terms):
            inner[w, at, :] = (dot_abt(gath[at, :], ops[h, w]) * gain).astype(BF)

    def apply_second(at, h):
        acc = dot_ab(ops[1 - h, 0, at, :], inner[0])
        for w in range(1, terms):
            acc = acc + dot_ab(ops[1 - h, w, at, :], inner[w])
        return acc

    def add_up(h, out, late):
        s1_out[...] = apply_second(other, h).astype(BF)
        pair = remote(s1_out, s1_in, s1_sem.at[0], s1_sem.at[1], buddy)
        pair.start()
        own[...] = apply_second(ours, h)
        sent(out)
        pair.wait_recv()
        pieces = [None] * 3
        for i in (1, 0, 2):
            to = rows(lax.rem(y + 1 + i, NY), slim)
            s2_out[i] = (own[to, :] + s1_in[to, :].astype(F32)).astype(BF)
            pieces[i] = remote(s2_out.at[i], s2_in.at[i], s2_ss.at[i], s2_rs.at[i], chip(i + 1))
            pieces[i].start()
        total = own[rows(y, slim), :] + s1_in[rows(y, slim), :].astype(F32)
        late()
        for i in (0, 2, 1):
            pieces[i].wait_recv()
            total = total + s2_in[i].astype(F32)
        pair.wait_send()
        for piece in pieces:
            piece.wait_send()
        return total.astype(BF)

    def advance(line, applied, gain, live_row, live_col):
        x = masked(2.0 * state[...] - applied * gain, live_row, live_col)
        state[...] = x
        note(line, x)

    cols = lambda yy: gath.at[:, rows(yy, wide)]
    norm_view = lambda c, yy: norms.at[c, yy]
    env_view = lambda c, yy: env.at[c, rows(yy, wide)]

    def from_this_core(view, ss, rs):
        def copy(i):
            block = view(core, y if i < 4 else lax.rem(y + NY - 1 - (i - 4), NY))
            return remote(block, block, ss.at[i], rs.at[i], chip(i + 1) if i < 3 else buddy)

        def start():
            for i in (1, 0, 2, 3):
                copy(i).start()

        def forward():
            for i in (0, 2, 1):
                copy(i).wait_recv()
                copy(4 + i).start()

        def arrive():
            for i in range(3, 7):
                block = view(1 - core, y if i < 4 else lax.rem(y + NY - 1 - (i - 4), NY))
                remote(block, block, ss.at[i], rs.at[i], buddy).wait_recv()

        def finish():
            for i in range(7):
                copy(i).wait_send()

        return start, forward, arrive, finish

    norm_start, norm_forward, norm_arrive, norm_finish = from_this_core(norm_view, norm_ss, norm_rs)
    env_start, env_forward, env_arrive, env_finish = from_this_core(env_view, env_ss, env_rs)
    col_start, col_forward, col_arrive, col_finish = from_this_core(lambda c, yy: cols(yy), early_ss, early_rs)

    def set_scale(h):
        peaks = [norms[h, i, 0, 0:1, 0:1] for i in range(NY)]
        top = functools.reduce(jnp.maximum, peaks)
        whole = jnp.zeros((1, 1), F32)
        for i in range(NY):
            ratio = peaks[i] / top
            whole = whole + norms[h, i, 1, 0:1, 0:1] * (ratio * ratio)
        env_scale[h] = jnp.broadcast_to(root / (top * jnp.sqrt(whole + EPS)), (8, 128))

    def spread_env():
        @pl.when(core == 0)
        def _():
            env_forward()

    @pl.when(core == 0)
    def _():
        gath[:, mine] = dot_abt(unit[...], env[0, mine, :]).astype(BF)
        norm_start()
        col_start()
        norm_forward()

    @pl.when(core == 1)
    def _():
        norm_arrive()

    set_scale(0)

    @pl.when(core == 0)
    def _():
        col_forward()
        env_start()

    @pl.when(core == 1)
    def _():
        col_arrive()

    load_l.wait()
    gain = env_scale[0, 0:1, 0:1]
    apply_first(ours, 0, gain)
    apply_first(other, 0, gain)

    @pl.when(core == 0)
    def _():
        col_finish()

    load_r.wait()
    total = add_up(0, [], spread_env)

    @pl.when(core == 1)
    def _():
        env_arrive()

    advance(1, dot_ab(total, env[0]), gain, rank1, rank0)

    def iteration(n, _):
        h = lax.div(n, ITERS)

        @pl.when(n == ITERS)
        def _():
            turn()

        gain = env_scale[h, 0:1, 0:1]
        x = state[...].astype(BF)

        @pl.when(h == 0)
        def _():
            gath[my_rows, :] = (dot_abt(x, env[0]) * gain).astype(BF)

        @pl.when(h == 1)
        def _():
            gath[my_rows, :] = (dot_ab(x, env[1]) * gain).astype(BF)

        out = spread_out(gath_view, gath_ss, gath_rs)
        pass_on(gath_view, out, gath_ss, gath_rs)

        @pl.when((n == 1) & (core == 1))
        def _():
            env_start()
            norm_start()

        apply_first(ours, h, 1.0)
        rest(out)
        apply_first(other, h, 1.0)
        total = add_up(h, out, lambda: None)

        @pl.when(h == 0)
        def _():
            advance(1 + n, dot_ab(total, env[0]), gain, rank1, rank0)

            @pl.when(core == 1)
            def _():
                env_forward()
                norm_forward()

        @pl.when(h == 1)
        def _():
            advance(1 + n - ITERS, dot_abt(total, env[1]), gain, rank0, rank1)

        return 0

    lax.fori_loop(1, 2 * ITERS, iteration, 0)
    env_finish()
    norm_finish()
    total = collect()
    scale = overall(total, float(blk) / jnp.sqrt(total[0:1, 0:1] + EPS))
    out_ref[...] = state_all[...].astype(F32) * scale


def per_device(nseg, left_blocks, right_blocks, start_state, left_transfer, right_transfer, ranks):
    blk, terms = left_blocks.shape[-1], left_blocks.shape[1]
    half, wide, slim = blk // 2, blk // NY, blk // (2 * NY)
    dma = pltpu.SemaphoreType.DMA
    scratch = [
        pltpu.VMEM((2, terms, blk, blk), BF),
        pltpu.SMEM((1, 2), jnp.int32),
        pltpu.VMEM((blk, blk), F32),
        pltpu.VMEM((blk, blk), F32),
        pltpu.VMEM((blk, blk), BF),
        pltpu.VMEM((4 + nseg // 8, PIECES, wide // PIECES, blk), BF),
        pltpu.VMEM((2 + nseg // 8, PIECES, wide // PIECES, blk), BF),
        pltpu.VMEM((2, blk, blk), BF),
        pltpu.VMEM((2, blk, blk), BF),
        pltpu.VMEM((2, 8, 128), F32),
        pltpu.VMEM((2, NY, 2, 8, 128), F32),
        pltpu.VMEM((blk, blk), BF),
        pltpu.VMEM((terms, blk, blk), BF),
        pltpu.VMEM((half, blk), F32),
        pltpu.VMEM((half, blk), BF),
        pltpu.VMEM((half, blk), BF),
        pltpu.VMEM((3, slim, blk), BF),
        pltpu.VMEM((3, slim, blk), BF),
        pltpu.VMEM((slim, blk), F32),
        pltpu.VMEM((8, 128), F32),
        pltpu.VMEM((blk, blk), BF),
        pltpu.VMEM((2 * NY, 8, 128), F32),
        pltpu.VMEM((2 * slim, blk), F32),
        pltpu.VMEM((blk, 2 * slim), BF),
        pltpu.VMEM((2, 2 * NY, slim, 2 * slim), BF),
        pltpu.VMEM((2 * blk, blk), BF),
        dma((5,)),
        dma((4 + nseg // 8, PIECES)), dma((4 + nseg // 8, PIECES)),
        dma((2, 3)), dma((2, 3)),
        dma((7,)), dma((7,)),
        dma((7,)), dma((7,)),
        dma((7,)), dma((7,)),
        dma((7,)), dma((7,)),
        dma((7,)), dma((7,)),
        dma((7,)), dma((7,)),
        dma((2,)),
        dma((3,)), dma((3,)),
        dma((4 * NY,)), dma((4 * NY,)),
        pltpu.SemaphoreType.REGULAR,
    ]
    hbm = pl.BlockSpec(memory_space=pltpu.HBM)
    final = pl.pallas_call(
        functools.partial(kernel, nseg, blk, terms),
        out_shape=jax.ShapeDtypeStruct((blk, blk), F32),
        in_specs=[hbm] * 6,
        out_specs=pl.BlockSpec(memory_space=pltpu.VMEM),
        scratch_shapes=scratch,
        compiler_params=pltpu.CompilerParams(
            collective_id=0, has_side_effects=True, vmem_limit_bytes=52 * 1024 * 1024
        ),
        name="dmrg",
    )(left_blocks, right_blocks, start_state, left_transfer, right_transfer, ranks)
    return final[None]


def solution(mesh):
    in_specs = (
        P("seg", "term", None, None),
        P("seg", "term", None, None),
        P("seg", None, None),
        P("seg", None, None),
        P("seg", None, None),
        P("seg", None),
    )
    out_specs = P("seg", None, None)
    return jax.shard_map(
        functools.partial(per_device, mesh.shape["seg"]),
        mesh=mesh, in_specs=in_specs, out_specs=out_specs, check_vma=False,
    )
```
